256 devices in a mesh: seq: 128 (over z, x, y_lo, core), tp: 2 (over y_hi).
Axes of the slice: x: 4, y: 4 (y_hi: 2, y_lo: 2; y = y_hi * 2 + y_lo), z: 8, core: 2. Of those that a mesh axis runs over, the one named last changes fastest.
Arguments:
- video_latent: bfloat16 [128, 256, 1152], P('seq'), may hold values from -6 to 6
- shift_temporal: float32 [1152], replicated, may hold values from -3 to 3
- scale_temporal: float32 [1152], replicated, may hold values from -0.5 to 3
- gate_temporal: float32 [1152], replicated, may hold values from 0.4 to 1.6
- temporal_qkv: bfloat16 [1152, 3, 1152], P(None, None, 'tp'), may hold values from -0.1875 to 0.1875
- temporal_proj: bfloat16 [1152, 1152], P('tp'), may hold values from -0.1875 to 0.1875
- cross_query: bfloat16 [1152, 1152], P(None, 'tp'), may hold values from -0.1875 to 0.1875
- cross_kv: bfloat16 [2, 4096, 1152], P(None, 'seq', 'tp'), may hold values from -0.09375 to 0.09375
- cross_proj: bfloat16 [1152, 1152], P('tp'), may hold values from -0.1875 to 0.1875
- text_embed: bfloat16 [300, 4096], P(None, 'seq'), may hold values from -25 to 25, as said below
- text_length: int32 [1], replicated, may hold values from 75 to 300
Outputs:
- block_out: float32 [128, 256, 1152], P('seq')
The draws below stay inside these ranges and needn't reach their ends.
Inputs may be any that keep to these rules, and one draw needn't show every extreme that they name: `text_embed`: text states, of varied scale over features.
All inputs are finite; a program needn't handle non-finite values.
Results may differ from the reference program's by a relative error of at most 0.025.
Values may be sent and summed in bfloat16 or wider, within the bound.
A program may use at most 128 MiB of HBM per device.

```python
import math
import jax
import jax.numpy as jnp
from jax import lax

D = 1152
HEADS = 16
HD = 72
TEXT_D = 4096
TEXT_LEN = 300
LOCS = 256
FRAMES = 128


def draw_scale_temporal(key, part):
    key = jax.random.fold_in(key, 11)
    return jax.random.uniform(key, (D,), jnp.float32, -0.5, 1.0)


def draw_text_embed(key, part):
    key = jax.random.fold_in(key, 23)
    first, second, third = jax.random.split(key, 3)
    column_scale = 10.0 ** jax.random.uniform(first, (TEXT_D,), jnp.float32, -0.5, 0.5)
    row_scale = 10.0 ** jax.random.uniform(second, (TEXT_LEN, 1), jnp.float32, -0.25, 0.25)
    base = jnp.clip(jax.random.normal(third, (TEXT_LEN, TEXT_D), jnp.float32), -4.0, 4.0)
    return (base * row_scale * column_scale[None, :]).astype(jnp.bfloat16)


def levels(rng, dims, pieces, smallest, high):
    factor_of, own = 1.0, jax.random.fold_in(rng, 6)
    for axis_at, blocks in pieces:
        heights = jnp.exp(jax.random.uniform(jax.random.fold_in(own, axis_at), (blocks,), jnp.float32, smallest / len(pieces), high / len(pieces)))
        factor_of = factor_of * jnp.repeat(heights, dims[axis_at] // blocks).reshape([-1 if axis == axis_at else 1 for axis in range(len(dims))])
    return factor_of


def noise(stream_key, extent, scale, reach, cuts=(), held_as=jnp.bfloat16):
    factor_of = levels(stream_key, extent, cuts, -0.22, 0.18) if cuts else 1.0
    drawn = jax.random.normal(stream_key, extent, jnp.float32) * scale * factor_of
    return jnp.minimum(jnp.maximum(drawn, -reach), reach).astype(held_as)


def setup_inputs(seed: int = 0) -> dict:
    arg_keys = jax.random.split(jax.random.key(seed), 12)
    return {
        "video_latent": noise(arg_keys[0], (FRAMES, LOCS, D), 1.0, 6.0, ((0, 128),)),
        "shift_temporal": noise(arg_keys[1], (D,), 0.5, 3.0, (), jnp.float32),
        "scale_temporal": draw_scale_temporal(jax.random.fold_in(arg_keys[11], 71), 0),
        "gate_temporal": jnp.clip(jax.random.uniform(arg_keys[3], (D,), jnp.float32, 0.4, 1.6), 0.4, 1.6),
        "temporal_qkv": noise(arg_keys[4], (D, 3, HEADS * HD), D ** -0.5, 0.1875, ((2, 2),)),
        "temporal_proj": noise(arg_keys[5], (HEADS * HD, D), (HEADS * HD) ** -0.5, 0.1875, ((0, 2),)),
        "cross_query": noise(arg_keys[6], (D, HEADS * HD), D ** -0.5, 0.1875, ((1, 2),)),
        "cross_kv": noise(arg_keys[7], (2, TEXT_D, HEADS * HD), TEXT_D ** -0.5, 0.09375, ((1, 128), (2, 2))),
        "cross_proj": noise(arg_keys[8], (HEADS * HD, D), (HEADS * HD) ** -0.5, 0.1875, ((0, 2),)),
        "text_embed": draw_text_embed(jax.random.fold_in(arg_keys[11], 71), 0),
        "text_length": jax.random.randint(arg_keys[10], (1,), TEXT_LEN // 4, TEXT_LEN + 1).astype(jnp.int32),
    }


def layer_norm(values):
    center = lax.optimization_barrier(jnp.mean(values, axis=-1, keepdims=True))
    spread = lax.optimization_barrier(jnp.mean(jnp.square(values - center), axis=-1, keepdims=True))
    return (values - center) * lax.rsqrt(spread + 1e-06)

def temporal_mix(projected):
    query_rows = projected[:, :, 0].astype(jnp.float32)
    key_rows = projected[:, :, 1].astype(jnp.float32)
    value_rows = projected[:, :, 2].astype(jnp.float32)
    scores = jnp.einsum('flhd,glhd->lhfg', query_rows, key_rows) * HD ** (-0.5)
    weights = jax.nn.softmax(scores, axis=-1).astype(jnp.bfloat16)
    return jnp.einsum('lhfg,glhd->flhd', weights.astype(jnp.float32), value_rows).astype(jnp.bfloat16)

def cross_mix(query_rows, key_rows, value_rows, length):
    scores = jnp.einsum('rhd,thd->rht', query_rows.astype(jnp.float32), key_rows, precision=lax.Precision.HIGHEST) * HD ** (-0.5)
    visible = jnp.arange(TEXT_LEN, dtype=jnp.int32) < length
    scores = jnp.where(visible[None, None, :], scores, -1e+30)
    weights = jax.nn.softmax(scores, axis=-1).astype(jnp.bfloat16)
    return jnp.einsum('rht,thd->rhd', weights.astype(jnp.float32), value_rows, precision=lax.Precision.HIGHEST).astype(jnp.bfloat16)

def reference(video_latent, shift_temporal, scale_temporal, gate_temporal, temporal_qkv, temporal_proj, cross_query, cross_kv, cross_proj, text_embed, text_length):
    width = HEADS * HD
    text_kv = jnp.einsum('tr,krc->ktc', text_embed.astype(jnp.float32), cross_kv.astype(jnp.float32), precision=lax.Precision.HIGHEST)
    text_kv = text_kv.reshape(2, TEXT_LEN, HEADS, HD)
    qkv_flat = temporal_qkv.reshape(D, 3 * width)
    blocksize = math.gcd(LOCS, 32)
    grouped = video_latent.reshape(FRAMES, LOCS // blocksize, blocksize, D).transpose(1, 0, 2, 3)

    def one_block(slab):
        tokens_f = slab.reshape(-1, D).astype(jnp.float32)
        normed = (layer_norm(tokens_f) * (1.0 + scale_temporal) + shift_temporal).astype(jnp.bfloat16)
        projected = jnp.dot(normed, qkv_flat, preferred_element_type=jnp.float32).astype(jnp.bfloat16)
        projected = projected.reshape(FRAMES, blocksize, 3, HEADS, HD)
        attended = temporal_mix(projected)
        temporal_out = jnp.dot(attended.reshape(-1, width), temporal_proj, preferred_element_type=jnp.float32)
        mixed = tokens_f + gate_temporal * temporal_out
        mixed_in = mixed.astype(jnp.bfloat16)
        query_rows = jnp.dot(mixed_in, cross_query, preferred_element_type=jnp.float32).astype(jnp.bfloat16)
        crossed = cross_mix(query_rows.reshape(-1, HEADS, HD), text_kv[0], text_kv[1], text_length[0])
        cross_out = jnp.dot(crossed.reshape(-1, width), cross_proj, preferred_element_type=jnp.float32)
        return (mixed + cross_out).reshape(FRAMES, blocksize, D)
    result = lax.map(one_block, grouped)
    return result.transpose(1, 0, 2, 3).reshape(FRAMES, LOCS, D)
```

```python
import jax
import jax.numpy as jnp
from jax import lax
from jax.experimental import pallas as pl
from jax.experimental.pallas import tpu as pltpu
from jax.sharding import PartitionSpec as P

D = 1152
HD = 72
HEADS = 8
WIDTH = HEADS * HD
TOKENS = 256
NZ = 8
NQ = 16
TEXT_ROWS = 304
EXP_SCALE = HD ** (-0.5) * 1.4426950408889634
MESH = pl.DeviceIdType.MESH


def rows_of(index, size):
    return pl.ds(pl.multiple_of(index * size, size), size)


def attend(query, key, value, visible, store):
    tiles = [None] * 5
    for head in range(HEADS):
        low, high = head * HD, (head + 1) * HD
        first, last = low // 128, (high - 1) // 128
        start, end = first * 128, min((last + 1) * 128, WIDTH)
        rows = query[:, start:end]
        lane = lax.broadcasted_iota(jnp.int32, rows.shape, 1) + start
        rows = jnp.where((lane >= low) & (lane < high), rows, jnp.zeros_like(rows))
        scores = lax.dot_general(
            rows, key[:, start:end], (((1,), (1,)), ((), ())), preferred_element_type=jnp.float32
        )
        scores = jnp.where(visible, scores, -1e30)
        top = jnp.max(scores, axis=-1, keepdims=True)
        weights = jnp.exp2((scores - top) * EXP_SCALE)
        total = jnp.sum(weights, axis=-1, keepdims=True)
        mixed = jnp.dot(
            weights.astype(jnp.bfloat16), value[:, start:end], preferred_element_type=jnp.float32
        ) * (1.0 / total)
        for tile in range(first, last + 1):
            piece = mixed[:, tile * 128 - start : min((tile + 1) * 128, WIDTH) - start]
            if tiles[tile] is not None:
                lane = lax.broadcasted_iota(jnp.int32, piece.shape, 1) + tile * 128
                piece = jnp.where(lane >= low, piece, tiles[tile])
            tiles[tile] = piece
            if high >= min((tile + 1) * 128, WIDTH):
                store(tile, piece.astype(jnp.bfloat16))


def kernel(
    length_ref, x_ref, shift_ref, scale_ref, gate_ref, wqkv_hbm, wp_hbm, wcq_hbm, wcp_hbm, tk_ref, tv_ref,
    out_ref,
    wqkv, wp, wp_far, wcq, wcp, wcp_far,
    s1, t32, msg, xin, normed, qkv, att, att_far, branch, o2, om, o1,
    load_sem, w_send, w_recv, s1_send, s1_recv, s2_send, s2_recv,
    a_send, a_recv, o2_send, o2_recv, o1_send, o1_recv,
):
    seq, hi = lax.axis_index("seq"), lax.axis_index("tp")
    z, q = seq // NQ, lax.rem(seq, NQ)
    core, spot = lax.rem(q, 2), q // 2

    def other_y(index):
        return index + 2 - 4 * lax.rem(index // 2, 2)

    def group_of(index):
        return index + hi * (other_y(index) - index)

    def place_of(index):
        group = group_of(index)
        return lax.rem(group, 2) * 8 + group // 2

    def at_z(index):
        return (index * NQ + q, hi)

    def at_q(index):
        return (z * NQ + index, hi)

    pair = (z * NQ + other_y(q), 1 - hi)
    sibling = at_q(q + 1 - 2 * core)

    loads = [
        pltpu.make_async_copy(source, target, load_sem.at[n])
        for n, (source, target) in enumerate(
            ((wqkv_hbm, wqkv), (wp_hbm, wp), (wcq_hbm, wcq), (wcp_hbm, wcp))
        )
    ]
    for load in loads:
        load.start()

    barrier = pltpu.get_barrier_semaphore()
    for step in range(1, NZ):
        pl.semaphore_signal(barrier, inc=1, device_id=at_z(lax.rem(z + step, NZ)), device_id_type=MESH)
    for step in range(1, NQ):
        pl.semaphore_signal(barrier, inc=1, device_id=at_q(lax.rem(q + step, NQ)), device_id_type=MESH)
    pl.semaphore_signal(barrier, inc=1, device_id=pair, device_id_type=MESH)
    pl.semaphore_wait(barrier, NZ - 1 + NQ - 1 + 1)

    def remote(source, target, send, recv, device):
        return pltpu.make_async_remote_copy(
            src_ref=source, dst_ref=target, send_sem=send, recv_sem=recv, device_id=device, device_id_type=MESH
        )

    sent = []

    for half in range(2):
        for n, step in enumerate((4, 3, 5, 2, 6, 1, 7)):
            target = lax.rem(z + step, NZ)
            copy = remote(
                x_ref.at[pl.ds(pl.multiple_of(target * 32 + half * 16, 16), 16)],
                s1.at[z, half], s1_send.at[n, half], s1_recv.at[z, half], at_z(target),
            )
            copy.start()
            sent.append(copy)
    half_rows = pl.ds(pl.multiple_of(core * 288, 288), 288)
    for n, (source, target) in enumerate(((wp_hbm, wp_far), (wcp_hbm, wcp_far))):
        copy = remote(source.at[half_rows], target.at[half_rows], w_send.at[n], w_recv.at[n], pair)
        copy.start()
        sent.append(copy)
    for half in range(2):
        s1[z, half] = x_ref[pl.ds(pl.multiple_of(z * 32 + half * 16, 16), 16)]

    for half in range(2):
        for step in range(1, NZ):
            source = lax.rem(z + step, NZ)
            remote(s1.at[source, half], s1.at[source, half], s1_send.at[0, half], s1_recv.at[source, half], at_z(source)).wait_recv()
        def spread_in(tile, carry):
            lanes = pl.ds(pl.multiple_of(tile * 128, 128), 128)
            for n in range(NZ):
                t32[n * 16 : (n + 1) * 16] = s1[n, half, :, lanes].astype(jnp.float32)
            for n in range(8):
                first = t32[pl.ds(2 * n, 8, stride=16), :]
                second = t32[pl.ds(2 * n + 1, 8, stride=16), :]
                msg[half * 8 + n, :, lanes] = jnp.concatenate([first, second], axis=0).astype(jnp.bfloat16)
            return carry

        lax.fori_loop(0, D // 128, spread_in, 0)
        for step in range(8):
            dest = 2 * lax.rem(spot + step, 8) + half
            copy = remote(msg.at[place_of(dest)], xin.at[q], s2_send.at[half * 8 + step], s2_recv.at[q], at_q(dest))
            if step:
                copy.start()
            else:
                pl.when(core != half)(copy.start)
            sent.append((copy, core != half) if step == 0 else copy)
    xin[q] = msg[place_of(q)]
    for step in range(1, NQ):
        source = lax.rem(q + step, NQ)
        remote(xin.at[source], xin.at[source], s2_send.at[0], s2_recv.at[source], at_q(source)).wait_recv()

    def norm_rows(n, carry):
        values = xin[n].astype(jnp.float32)
        center = jnp.mean(values, axis=-1, keepdims=True)
        values = values - center
        spread = jnp.mean(jnp.square(values), axis=-1, keepdims=True)
        values = values * lax.rsqrt(spread + 1e-06) * (1.0 + scale_ref[...]) + shift_ref[...]
        normed[rows_of(n, 16)] = values.astype(jnp.bfloat16)
        return carry

    lax.fori_loop(0, NQ, norm_rows, 0)
    loads[0].wait()

    def project(n, carry):
        qkv[n] = jnp.dot(normed[...], wqkv[n], preferred_element_type=jnp.float32).astype(jnp.bfloat16)
        return carry

    lax.fori_loop(0, 3, project, 0)

    for n, target in enumerate((wp_far, wcp_far)):
        remote(target.at[half_rows], target.at[half_rows], w_send.at[n], w_recv.at[n], pair).wait_recv()
        copy = remote(target.at[half_rows], target.at[half_rows], w_send.at[2 + n], w_recv.at[2 + n], sibling)
        copy.start()
        sent.append(copy)

    row = lax.broadcasted_iota(jnp.int32, (TOKENS, TOKENS), 0)
    column = lax.broadcasted_iota(jnp.int32, (TOKENS, TOKENS), 1)
    same = lax.rem(row // 8, 2) == lax.rem(column // 8, 2)

    def put(target):
        def store(tile, piece):
            target[:, tile * 128 : tile * 128 + piece.shape[1]] = piece

        return store

    attend(qkv.at[0], qkv.at[1], qkv.at[2], same, put(att.at[0]))
    swap = remote(att.at[0], att_far.at[0], a_send.at[0], a_recv.at[0], pair)
    swap.start()
    sent.append(swap)
    loads[1].wait()
    branch[...] = jnp.dot(att[0], wp[...], preferred_element_type=jnp.float32)
    other_rows = pl.ds(pl.multiple_of(288 - core * 288, 288), 288)
    remote(wp_far.at[other_rows], wp_far.at[other_rows], w_send.at[2], w_recv.at[2], sibling).wait_recv()
    swap.wait_recv()
    branch[...] = (branch[...] + jnp.dot(att_far[0], wp_far[...], preferred_element_type=jnp.float32)) * gate_ref[...]

    def mix_rows(n, carry):
        rows = rows_of(n, 16)
        normed[rows] = (xin[n].astype(jnp.float32) + branch[rows]).astype(jnp.bfloat16)
        return carry

    lax.fori_loop(0, NQ, mix_rows, 0)
    loads[2].wait()
    qkv[0] = jnp.dot(normed[...], wcq[...], preferred_element_type=jnp.float32).astype(jnp.bfloat16)
    text = lax.broadcasted_iota(jnp.int32, (1, TEXT_ROWS), 1)
    attend(qkv.at[0], tk_ref, tv_ref, text < length_ref[0], put(att.at[1]))
    swap = remote(att.at[1], att_far.at[1], a_send.at[1], a_recv.at[1], pair)
    swap.start()
    sent.append(swap)
    loads[3].wait()
    branch[...] += jnp.dot(att[1], wcp[...], preferred_element_type=jnp.float32)
    remote(wcp_far.at[other_rows], wcp_far.at[other_rows], w_send.at[3], w_recv.at[3], sibling).wait_recv()
    swap.wait_recv()
    branch[...] += jnp.dot(att_far[1], wcp_far[...], preferred_element_type=jnp.float32)

    def drain():
        for copy in sent:
            if isinstance(copy, tuple):
                pl.when(copy[1])(copy[0].wait_send)
            else:
                copy.wait_send()
        sent.clear()

    drain()

    for n in range(NQ):
        om[n] = branch[n * 16 : (n + 1) * 16].astype(jnp.bfloat16)
    place = place_of(q)
    for step in range(1, NQ):
        dest = lax.rem(q + step, NQ)
        copy = remote(
            om.at[dest], o2.at[place], o2_send.at[step], o2_recv.at[place], at_q(dest),
        )
        copy.start()
        sent.append(copy)
    o2[place] = om[q]
    for half in range(2):
        for step in range(8):
            source = 2 * lax.rem(spot + step, 8) + half
            slot = place_of(source)
            copy = remote(o2.at[slot], o2.at[slot], o2_send.at[0], o2_recv.at[slot], at_q(source))
            if step:
                copy.wait_recv()
            else:
                pl.when(core != half)(copy.wait_recv)
        def spread_out(tile, carry):
            lanes = pl.ds(pl.multiple_of(tile * 128, 128), 128)
            for n in range(8):
                t32[n * 16 : (n + 1) * 16] = o2[half * 8 + n, :, lanes].astype(jnp.float32)
            for n in range(NZ):
                msg[2 * n + half, :, lanes] = t32[pl.ds(n, 16, stride=8), :].astype(jnp.bfloat16)
            return carry

        lax.fori_loop(0, D // 128, spread_out, 0)
        for n, step in enumerate((4, 3, 5, 2, 6, 1, 7)):
            target = lax.rem(z + step, NZ)
            copy = remote(
                msg.at[2 * target + half], o1.at[2 * z + half], o1_send.at[n, half], o1_recv.at[z, half], at_z(target)
            )
            copy.start()
            sent.append(copy)
        o1[2 * z + half] = msg[2 * z + half]
    for half in range(2):
        for step in range(1, NZ):
            source = lax.rem(z + step, NZ)
            remote(o1.at[2 * source + half], o1.at[2 * source + half], o1_send.at[0, half], o1_recv.at[source, half], at_z(source)).wait_recv()

    def finish(n, carry):
        rows = rows_of(n, 16)
        out_ref[rows] = x_ref[rows].astype(jnp.float32) + o1[n].astype(jnp.float32)
        return carry

    lax.fori_loop(0, NQ, finish, 0)
    drain()


def mega(length, x, shift, scale, gate, wqkv, wp, wcq, wcp, tk, tv):
    vmem = pl.BlockSpec(memory_space=pltpu.VMEM)
    hbm = pl.BlockSpec(memory_space=pl.ANY)
    bf16, f32 = jnp.bfloat16, jnp.float32
    dma = pltpu.SemaphoreType.DMA
    return pl.pallas_call(
        kernel,
        out_shape=jax.ShapeDtypeStruct((TOKENS, D), f32),
        in_specs=[pl.BlockSpec(memory_space=pltpu.SMEM), vmem, vmem, vmem, vmem, hbm, hbm, hbm, hbm, vmem, vmem],
        out_specs=vmem,
        scratch_shapes=[
            pltpu.VMEM((3, D, WIDTH), bf16),
            pltpu.VMEM((WIDTH, D), bf16),
            pltpu.VMEM((WIDTH, D), bf16),
            pltpu.VMEM((D, WIDTH), bf16),
            pltpu.VMEM((WIDTH, D), bf16),
            pltpu.VMEM((WIDTH, D), bf16),
            pltpu.VMEM((NZ, 2, 16, D), bf16),
            pltpu.VMEM((128, 128), f32),
            pltpu.VMEM((16, 16, D), bf16),
            pltpu.VMEM((16, 16, D), bf16),
            pltpu.VMEM((TOKENS, D), bf16),
            pltpu.VMEM((3, TOKENS, WIDTH), bf16),
            pltpu.VMEM((2, TOKENS, WIDTH), bf16),
            pltpu.VMEM((2, TOKENS, WIDTH), bf16),
            pltpu.VMEM((TOKENS, D), f32),
            pltpu.VMEM((16, 16, D), bf16),
            pltpu.VMEM((16, 16, D), bf16),
            pltpu.VMEM((16, 16, D), bf16),
            dma((4,)), dma((4,)), dma((4,)),
            dma((7, 2)), dma((8, 2)), dma((16,)), dma((16,)),
            dma((2,)), dma((2,)), dma((16,)), dma((16,)), dma((7, 2)), dma((8, 2)),
        ],
        compiler_params=pltpu.CompilerParams(
            collective_id=0, has_side_effects=True, vmem_limit_bytes=48 * 1024 * 1024
        ),
        cost_estimate=pl.CostEstimate(flops=4_000_000_000, bytes_accessed=12_000_000, transcendentals=2_000_000),
        name="stdit",
    )(length, x, shift, scale, gate, wqkv, wp, wcq, wcp, tk, tv)


def body(
    video_latent, shift_temporal, scale_temporal, gate_temporal, temporal_qkv, temporal_proj,
    cross_query, cross_kv, cross_proj, text_embed, text_length,
):
    partial = jnp.einsum("tr,krc->ktc", text_embed, cross_kv, preferred_element_type=jnp.float32)
    text_kv = lax.psum(partial, "seq").astype(jnp.bfloat16)
    text_kv = jnp.pad(text_kv, ((0, 0), (0, TEXT_ROWS - text_kv.shape[1]), (0, 0)))
    out = mega(
        text_length, video_latent.reshape(TOKENS, D),
        shift_temporal.reshape(1, D), scale_temporal.reshape(1, D), gate_temporal.reshape(1, D),
        jnp.transpose(temporal_qkv, (1, 0, 2)), temporal_proj, cross_query, cross_proj, text_kv[0], text_kv[1],
    )
    return out.reshape(1, TOKENS, D)


def solution(mesh):
    return jax.shard_map(
        body,
        mesh=mesh,
        in_specs=(
            P("seq", None, None), P(), P(), P(), P(None, None, "tp"), P("tp", None), P(None, "tp"),
            P(None, "seq", "tp"), P("tp", None), P(None, "seq"), P(),
        ),
        out_specs=P("seq", None, None),
        check_vma=False,
    )
```

```python
import jax
import jax.numpy as jnp
from jax import lax
from jax.experimental import pallas as pl
from jax.experimental.pallas import tpu as pltpu
from jax.sharding import PartitionSpec as P

D = 1152
HD = 72
HEADS = 8
WIDTH = HEADS * HD
TOKENS = 256
NZ = 8
NQ = 16
TEXT_LEN = 300
TEXT_ROWS = 304
EXP_SCALE = HD ** (-0.5) * 1.4426950408889634
MESH = pl.DeviceIdType.MESH


def rows_of(index, size):
    return pl.ds(pl.multiple_of(index * size, size), size)


def attend(query, key, value, visible, store):
    tiles = [None] * 5
    for head in range(HEADS):
        low, high = head * HD, (head + 1) * HD
        first, last = low // 128, (high - 1) // 128
        start, end = first * 128, min((last + 1) * 128, WIDTH)
        rows = query[:, start:end]
        lane = lax.broadcasted_iota(jnp.int32, rows.shape, 1) + start
        rows = jnp.where((lane >= low) & (lane < high), rows, jnp.zeros_like(rows))
        scores = lax.dot_general(
            rows, key[:, start:end], (((1,), (1,)), ((), ())), preferred_element_type=jnp.float32
        )
        scores = jnp.where(visible, scores, -1e30)
        top = jnp.max(scores, axis=-1, keepdims=True)
        weights = jnp.exp2((scores - top) * EXP_SCALE)
        total = jnp.sum(weights, axis=-1, keepdims=True)
        mixed = jnp.dot(
            weights.astype(jnp.bfloat16), value[:, start:end], preferred_element_type=jnp.float32
        ) * (1.0 / total)
        for tile in range(first, last + 1):
            piece = mixed[:, tile * 128 - start : min((tile + 1) * 128, WIDTH) - start]
            if tiles[tile] is not None:
                lane = lax.broadcasted_iota(jnp.int32, piece.shape, 1) + tile * 128
                piece = jnp.where(lane >= low, piece, tiles[tile])
            tiles[tile] = piece
            if high >= min((tile + 1) * 128, WIDTH):
                store(tile, piece.astype(jnp.bfloat16))


def across(rows, weights):
    return lax.dot_general(
        rows, weights, (((1,), (1,)), ((), ())), preferred_element_type=jnp.float32
    ).astype(jnp.bfloat16)


def kernel(
    length_ref, x_ref, shift_ref, scale_ref, gate_ref, wqkv_hbm, wp_hbm, wcq_hbm, wcp_hbm, ckv_ref, te_ref,
    out_ref,
    wqkv, wp, wp_far, wcq, wcp, wcp_far,
    s1, t32, msg, xin, normed, qkv, att, att_far, branch, o2, om, o1,
    te_pad, part, core_in, part_x, x_in, part_z, z_in, part_y, y_in, full, tk, tv,
    load_sem, w_send, w_recv, s1_send, s1_recv, s2_send, s2_recv,
    a_send, a_recv, o2_send, o2_recv, o1_send, o1_recv,
    c_send, c_recv, x_send, x_recv, z_send, z_recv, y_send, y_recv,
):
    seq, hi = lax.axis_index("seq"), lax.axis_index("tp")
    z, q = seq // NQ, lax.rem(seq, NQ)
    core, spot = lax.rem(q, 2), q // 2

    def other_y(index):
        return index + 2 - 4 * lax.rem(index // 2, 2)

    def group_of(index):
        return index + hi * (other_y(index) - index)

    def place_of(index):
        group = group_of(index)
        return lax.rem(group, 2) * 8 + group // 2

    def at_z(index):
        return (index * NQ + q, hi)

    def at_q(index):
        return (z * NQ + index, hi)

    def at_x(index):
        return at_q(index * 4 + lax.rem(q, 4))

    x = q // 4
    pair = (z * NQ + other_y(q), 1 - hi)
    sibling = at_q(q + 1 - 2 * core)

    loads = [
        pltpu.make_async_copy(source, target, load_sem.at[n])
        for n, (source, target) in enumerate(
            ((wqkv_hbm, wqkv), (wp_hbm, wp), (wcq_hbm, wcq), (wcp_hbm, wcp))
        )
    ]
    for load in loads:
        load.start()

    barrier = pltpu.get_barrier_semaphore()
    for step in range(1, NZ):
        pl.semaphore_signal(barrier, inc=1, device_id=at_z(lax.rem(z + step, NZ)), device_id_type=MESH)
    for step in range(1, NQ):
        pl.semaphore_signal(barrier, inc=1, device_id=at_q(lax.rem(q + step, NQ)), device_id_type=MESH)
    pl.semaphore_signal(barrier, inc=1, device_id=pair, device_id_type=MESH)
    pl.semaphore_wait(barrier, NZ - 1 + NQ - 1 + 1)

    def remote(source, target, send, recv, device):
        return pltpu.make_async_remote_copy(
            src_ref=source, dst_ref=target, send_sem=send, recv_sem=recv, device_id=device, device_id_type=MESH
        )

    sent = []

    def send(source, target, send_sem, recv_sem, device):
        copy = remote(source, target, send_sem, recv_sem, device)
        copy.start()
        sent.append(copy)

    def arrived(target, recv_sem, device):
        remote(target, target, c_send.at[0], recv_sem, device).wait_recv()

    def text_products():
        te_pad[...] = jnp.zeros_like(te_pad)
        te_pad[:, :TEXT_LEN] = te_ref[...]
        part[190:] = jnp.zeros((2, 16, 128), jnp.bfloat16)
        for which in range(2):
            product = lax.dot_general(
                te_pad[:, :TEXT_ROWS], ckv_ref[which], (((0,), (0,)), ((), ())), preferred_element_type=jnp.float32
            ).astype(jnp.bfloat16)
            product = jnp.concatenate([product, jnp.zeros((TEXT_ROWS, 64), jnp.bfloat16)], axis=1)
            for r in range(TEXT_ROWS // 16):
                for tile in range(5):
                    part[r * 10 + which * 5 + tile] = product[r * 16 : r * 16 + 16, tile * 128 : tile * 128 + 128]
        send(part.at[pl.ds(96 - 96 * core, 96)], core_in, c_send.at[0], c_recv.at[0], sibling)

    def text_core_sum():
        arrived(core_in, c_recv.at[0], sibling)
        part_x[...] = (part[pl.ds(96 * core, 96)].astype(jnp.float32) + core_in[...].astype(jnp.float32)).astype(jnp.bfloat16)
        for step in range(1, 4):
            target = lax.rem(x + step, 4)
            send(part_x.at[pl.ds(24 * target, 24)], x_in.at[x], x_send.at[0, step], x_recv.at[0, x], at_x(target))

    def text_x_sum():
        total = part_x[pl.ds(24 * x, 24)].astype(jnp.float32)
        for step in range(1, 4):
            source = lax.rem(x + step, 4)
            arrived(x_in.at[source], x_recv.at[0, source], at_x(source))
            total += x_in[source].astype(jnp.float32)
        part_z[...] = total.astype(jnp.bfloat16)
        for step in range(1, NZ):
            target = lax.rem(z + step, NZ)
            send(part_z.at[pl.ds(3 * target, 3)], z_in.at[z], z_send.at[0, step], z_recv.at[0, z], at_z(target))

    def text_z_sum():
        total = part_z[pl.ds(3 * z, 3)].astype(jnp.float32)
        for step in range(1, NZ):
            source = lax.rem(z + step, NZ)
            arrived(z_in.at[source], z_recv.at[0, source], at_z(source))
            total += z_in[source].astype(jnp.float32)
        part_y[...] = total.astype(jnp.bfloat16)
        send(part_y, y_in, y_send.at[0], y_recv.at[0], at_q(other_y(q)))

    def text_y_sum():
        arrived(y_in, y_recv.at[0], at_q(other_y(q)))
        mine = full.at[pl.ds(96 * core + 24 * x + 3 * z, 3)]
        mine[...] = (part_y[...].astype(jnp.float32) + y_in[...].astype(jnp.float32)).astype(jnp.bfloat16)
        for step in range(1, NZ):
            send(mine, mine, z_send.at[1, step], z_recv.at[1, z], at_z(lax.rem(z + step, NZ)))

    def text_z_gather():
        for step in range(1, NZ):
            source = lax.rem(z + step, NZ)
            arrived(full.at[pl.ds(96 * core + 24 * x + 3 * source, 3)], z_recv.at[1, source], at_z(source))
        mine = full.at[pl.ds(96 * core + 24 * x, 24)]
        for step in range(1, 4):
            send(mine, mine, x_send.at[1, step], x_recv.at[1, x], at_x(lax.rem(x + step, 4)))

    def text_x_gather():
        for step in range(1, 4):
            source = lax.rem(x + step, 4)
            arrived(full.at[pl.ds(96 * core + 24 * source, 24)], x_recv.at[1, source], at_x(source))
        mine = full.at[pl.ds(96 * core, 96)]
        send(mine, mine, c_send.at[1], c_recv.at[1], sibling)

    def text_core_gather():
        arrived(full.at[pl.ds(96 - 96 * core, 96)], c_recv.at[1], sibling)
        for which, target in enumerate((tk, tv)):
            for r in range(TEXT_ROWS // 16):
                for tile in range(5):
                    width = min(128, WIDTH - tile * 128)
                    target[r * 16 : r * 16 + 16, tile * 128 : tile * 128 + width] = full[r * 10 + which * 5 + tile][:, :width]

    for half in range(2):
        for n, step in enumerate((4, 3, 5, 2, 6, 1, 7)):
            target = lax.rem(z + step, NZ)
            copy = remote(
                x_ref.at[pl.ds(pl.multiple_of(target * 32 + half * 16, 16), 16)],
                s1.at[z, half], s1_send.at[n, half], s1_recv.at[z, half], at_z(target),
            )
            copy.start()
            sent.append(copy)
    half_rows = pl.ds(pl.multiple_of(core * 288, 288), 288)
    for n, (source, target) in enumerate(((wp_hbm, wp_far), (wcp_hbm, wcp_far))):
        copy = remote(source.at[half_rows], target.at[half_rows], w_send.at[n], w_recv.at[n], pair)
        copy.start()
        sent.append(copy)
    for half in range(2):
        s1[z, half] = x_ref[pl.ds(pl.multiple_of(z * 32 + half * 16, 16), 16)]

    text_products()

    for half in range(2):
        for step in range(1, NZ):
            source = lax.rem(z + step, NZ)
            remote(s1.at[source, half], s1.at[source, half], s1_send.at[0, half], s1_recv.at[source, half], at_z(source)).wait_recv()
        def spread_in(tile, carry):
            lanes = pl.ds(pl.multiple_of(tile * 128, 128), 128)
            for n in range(NZ):
                t32[n * 16 : (n + 1) * 16] = s1[n, half, :, lanes].astype(jnp.float32)
            for n in range(8):
                first = t32[pl.ds(2 * n, 8, stride=16), :]
                second = t32[pl.ds(2 * n + 1, 8, stride=16), :]
                msg[half * 8 + n, :, lanes] = jnp.concatenate([first, second], axis=0).astype(jnp.bfloat16)
            return carry

        lax.fori_loop(0, D // 128, spread_in, 0)
        for step in range(8):
            dest = 2 * lax.rem(spot + step, 8) + half
            copy = remote(msg.at[place_of(dest)], xin.at[q], s2_send.at[half * 8 + step], s2_recv.at[q], at_q(dest))
            if step:
                copy.start()
            else:
                pl.when(core != half)(copy.start)
            sent.append((copy, core != half) if step == 0 else copy)
        if half:
            text_x_sum()
        else:
            text_core_sum()
    xin[q] = msg[place_of(q)]
    for step in range(1, NQ):
        source = lax.rem(q + step, NQ)
        remote(xin.at[source], xin.at[source], s2_send.at[0], s2_recv.at[source], at_q(source)).wait_recv()

    def norm_rows(n, carry):
        values = xin[n].astype(jnp.float32)
        center = jnp.mean(values, axis=-1, keepdims=True)
        values = values - center
        spread = jnp.mean(jnp.square(values), axis=-1, keepdims=True)
        values = values * lax.rsqrt(spread + 1e-06) * (1.0 + scale_ref[...]) + shift_ref[...]
        normed[rows_of(n, 16)] = values.astype(jnp.bfloat16)
        return carry

    lax.fori_loop(0, NQ, norm_rows, 0)
    loads[0].wait()

    def project(n, carry):
        qkv[n] = across(normed[...], wqkv[n])
        return carry

    lax.fori_loop(0, 3, project, 0)

    text_z_sum()

    for n, target in enumerate((wp_far, wcp_far)):
        remote(target.at[half_rows], target.at[half_rows], w_send.at[n], w_recv.at[n], pair).wait_recv()
        copy = remote(target.at[half_rows], target.at[half_rows], w_send.at[2 + n], w_recv.at[2 + n], sibling)
        copy.start()
        sent.append(copy)

    row = lax.broadcasted_iota(jnp.int32, (TOKENS, TOKENS), 0)
    column = lax.broadcasted_iota(jnp.int32, (TOKENS, TOKENS), 1)
    same = lax.rem(row // 8, 2) == lax.rem(column // 8, 2)

    def put(target):
        def store(tile, piece):
            target[:, tile * 128 : tile * 128 + piece.shape[1]] = piece

        return store

    attend(qkv.at[0], qkv.at[1], qkv.at[2], same, put(att.at[0]))
    swap = remote(att.at[0], att_far.at[0], a_send.at[0], a_recv.at[0], pair)
    swap.start()
    sent.append(swap)
    text_y_sum()
    loads[1].wait()
    branch[...] = jnp.dot(att[0], wp[...], preferred_element_type=jnp.float32)
    other_rows = pl.ds(pl.multiple_of(288 - core * 288, 288), 288)
    remote(wp_far.at[other_rows], wp_far.at[other_rows], w_send.at[2], w_recv.at[2], sibling).wait_recv()
    text_z_gather()
    swap.wait_recv()
    branch[...] = (branch[...] + jnp.dot(att_far[0], wp_far[...], preferred_element_type=jnp.float32)) * gate_ref[...]

    def mix_rows(n, carry):
        rows = rows_of(n, 16)
        normed[rows] = (xin[n].astype(jnp.float32) + branch[rows]).astype(jnp.bfloat16)
        return carry

    lax.fori_loop(0, NQ, mix_rows, 0)
    text_x_gather()
    loads[2].wait()
    qkv[0] = across(normed[...], wcq[...])
    text_core_gather()
    text = lax.broadcasted_iota(jnp.int32, (1, TEXT_ROWS), 1)
    attend(qkv.at[0], tk, tv, text < length_ref[0], put(att.at[1]))
    swap = remote(att.at[1], att_far.at[1], a_send.at[1], a_recv.at[1], pair)
    swap.start()
    sent.append(swap)
    loads[3].wait()
    branch[...] += jnp.dot(att[1], wcp[...], preferred_element_type=jnp.float32)
    remote(wcp_far.at[other_rows], wcp_far.at[other_rows], w_send.at[3], w_recv.at[3], sibling).wait_recv()
    swap.wait_recv()
    branch[...] += jnp.dot(att_far[1], wcp_far[...], preferred_element_type=jnp.float32)

    def drain():
        for copy in sent:
            if isinstance(copy, tuple):
                pl.when(copy[1])(copy[0].wait_send)
            else:
                copy.wait_send()
        sent.clear()

    drain()

    for n in range(NQ):
        om[n] = branch[n * 16 : (n + 1) * 16].astype(jnp.bfloat16)
    place = place_of(q)
    for step in range(1, NQ):
        dest = lax.rem(q + step, NQ)
        copy = remote(
            om.at[dest], o2.at[place], o2_send.at[step], o2_recv.at[place], at_q(dest),
        )
        copy.start()
        sent.append(copy)
    o2[place] = om[q]
    for half in range(2):
        for step in range(8):
            source = 2 * lax.rem(spot + step, 8) + half
            slot = place_of(source)
            copy = remote(o2.at[slot], o2.at[slot], o2_send.at[0], o2_recv.at[slot], at_q(source))
            if step:
                copy.wait_recv()
            else:
                pl.when(core != half)(copy.wait_recv)
        def spread_out(tile, carry):
            lanes = pl.ds(pl.multiple_of(tile * 128, 128), 128)
            for n in range(8):
                t32[n * 16 : (n + 1) * 16] = o2[half * 8 + n, :, lanes].astype(jnp.float32)
            for n in range(NZ):
                msg[2 * n + half, :, lanes] = t32[pl.ds(n, 16, stride=8), :].astype(jnp.bfloat16)
            return carry

        lax.fori_loop(0, D // 128, spread_out, 0)
        for n, step in enumerate((4, 3, 5, 2, 6, 1, 7)):
            target = lax.rem(z + step, NZ)
            copy = remote(
                msg.at[2 * target + half], o1.at[2 * z + half], o1_send.at[n, half], o1_recv.at[z, half], at_z(target)
            )
            copy.start()
            sent.append(copy)
        o1[2 * z + half] = msg[2 * z + half]
    for half in range(2):
        for step in range(1, NZ):
            source = lax.rem(z + step, NZ)
            remote(o1.at[2 * source + half], o1.at[2 * source + half], o1_send.at[0, half], o1_recv.at[source, half], at_z(source)).wait_recv()

    def finish(n, carry):
        rows = rows_of(n, 16)
        out_ref[rows] = x_ref[rows].astype(jnp.float32) + o1[n].astype(jnp.float32)
        return carry

    lax.fori_loop(0, NQ, finish, 0)
    drain()


def mega(length, x, shift, scale, gate, wqkv, wp, wcq, wcp, ckv, te):
    vmem = pl.BlockSpec(memory_space=pltpu.VMEM)
    hbm = pl.BlockSpec(memory_space=pl.ANY)
    bf16, f32 = jnp.bfloat16, jnp.float32
    dma = pltpu.SemaphoreType.DMA
    return pl.pallas_call(
        kernel,
        out_shape=jax.ShapeDtypeStruct((TOKENS, D), f32),
        in_specs=[pl.BlockSpec(memory_space=pltpu.SMEM), vmem, vmem, vmem, vmem, hbm, hbm, hbm, hbm, vmem, vmem],
        out_specs=vmem,
        scratch_shapes=[
            pltpu.VMEM((3, WIDTH, D), bf16),
            pltpu.VMEM((WIDTH, D), bf16),
            pltpu.VMEM((WIDTH, D), bf16),
            pltpu.VMEM((WIDTH, D), bf16),
            pltpu.VMEM((WIDTH, D), bf16),
            pltpu.VMEM((WIDTH, D), bf16),
            pltpu.VMEM((NZ, 2, 16, D), bf16),
            pltpu.VMEM((128, 128), f32),
            pltpu.VMEM((16, 16, D), bf16),
            pltpu.VMEM((16, 16, D), bf16),
            pltpu.VMEM((TOKENS, D), bf16),
            pltpu.VMEM((3, TOKENS, WIDTH), bf16),
            pltpu.VMEM((2, TOKENS, WIDTH), bf16),
            pltpu.VMEM((2, TOKENS, WIDTH), bf16),
            pltpu.VMEM((TOKENS, D), f32),
            pltpu.VMEM((16, 16, D), bf16),
            pltpu.VMEM((16, 16, D), bf16),
            pltpu.VMEM((16, 16, D), bf16),
            pltpu.VMEM((32, 384), bf16),
            pltpu.VMEM((192, 16, 128), bf16),
            pltpu.VMEM((96, 16, 128), bf16),
            pltpu.VMEM((96, 16, 128), bf16),
            pltpu.VMEM((4, 24, 16, 128), bf16),
            pltpu.VMEM((24, 16, 128), bf16),
            pltpu.VMEM((8, 3, 16, 128), bf16),
            pltpu.VMEM((3, 16, 128), bf16),
            pltpu.VMEM((3, 16, 128), bf16),
            pltpu.VMEM((192, 16, 128), bf16),
            pltpu.VMEM((TEXT_ROWS, WIDTH), bf16),
            pltpu.VMEM((TEXT_ROWS, WIDTH), bf16),
            dma((4,)), dma((4,)), dma((4,)),
            dma((7, 2)), dma((8, 2)), dma((16,)), dma((16,)),
            dma((2,)), dma((2,)), dma((16,)), dma((16,)), dma((7, 2)), dma((8, 2)),
            dma((2,)), dma((2,)), dma((2, 4)), dma((2, 4)), dma((2, 8)), dma((2, 8)), dma((1,)), dma((1,)),
        ],
        compiler_params=pltpu.CompilerParams(
            collective_id=0, has_side_effects=True, vmem_limit_bytes=48 * 1024 * 1024
        ),
        cost_estimate=pl.CostEstimate(flops=4_000_000_000, bytes_accessed=12_000_000, transcendentals=2_000_000),
        name="stdit",
    )(length, x, shift, scale, gate, wqkv, wp, wcq, wcp, ckv, te)


def body(
    video_latent, shift_temporal, scale_temporal, gate_temporal, temporal_qkv, temporal_proj,
    cross_query, cross_kv, cross_proj, text_embed, text_length,
):
    out = mega(
        text_length, video_latent.reshape(TOKENS, D),
        shift_temporal.reshape(1, D), scale_temporal.reshape(1, D), gate_temporal.reshape(1, D),
        jnp.transpose(temporal_qkv, (1, 2, 0)), temporal_proj, cross_query.T, cross_proj, cross_kv, text_embed.T,
    )
    return out.reshape(1, TOKENS, D)


def solution(mesh):
    return jax.shard_map(
        body,
        mesh=mesh,
        in_specs=(
            P("seq", None, None), P(), P(), P(), P(None, None, "tp"), P("tp", None), P(None, "tp"),
            P(None, "seq", "tp"), P("tp", None), P(None, "seq"), P(),
        ),
        out_specs=P("seq", None, None),
        check_vma=False,
    )
```

```python
import jax
import jax.numpy as jnp
from jax import lax
from jax.experimental import pallas as pl
from jax.experimental.pallas import tpu as pltpu
from jax.sharding import PartitionSpec as P

D = 1152
HD = 72
HEADS = 8
WIDTH = HEADS * HD
TOKENS = 256
NZ = 8
NQ = 16
TEXT_LEN = 300
TEXT_ROWS = 304
EXP_SCALE = HD ** (-0.5) * 1.4426950408889634
MESH = pl.DeviceIdType.MESH


def rows_of(index, size):
    return pl.ds(pl.multiple_of(index * size, size), size)


def attend(query, key, value, visible, store):
    tiles = [None] * 5
    for head in range(HEADS):
        low, high = head * HD, (head + 1) * HD
        first, last = low // 128, (high - 1) // 128
        start, end = first * 128, min((last + 1) * 128, WIDTH)
        rows = query[:, start:end]
        lane = lax.broadcasted_iota(jnp.int32, rows.shape, 1) + start
        rows = jnp.where((lane >= low) & (lane < high), rows, jnp.zeros_like(rows))
        scores = lax.dot_general(
            rows, key[:, start:end], (((1,), (1,)), ((), ())), preferred_element_type=jnp.float32
        )
        scores = jnp.where(visible, scores, -1e30)
        top = jnp.max(scores, axis=-1, keepdims=True)
        weights = jnp.exp2((scores - top) * EXP_SCALE)
        total = jnp.sum(weights, axis=-1, keepdims=True)
        mixed = jnp.dot(
            weights.astype(jnp.bfloat16), value[:, start:end], preferred_element_type=jnp.float32
        ) * (1.0 / total)
        for tile in range(first, last + 1):
            piece = mixed[:, tile * 128 - start : min((tile + 1) * 128, WIDTH) - start]
            if tiles[tile] is not None:
                lane = lax.broadcasted_iota(jnp.int32, piece.shape, 1) + tile * 128
                piece = jnp.where(lane >= low, piece, tiles[tile])
            tiles[tile] = piece
            if high >= min((tile + 1) * 128, WIDTH):
                store(tile, piece.astype(jnp.bfloat16))


def across(rows, weights):
    return lax.dot_general(
        rows, weights, (((1,), (1,)), ((), ())), preferred_element_type=jnp.float32
    ).astype(jnp.bfloat16)


def kernel(
    length_ref, x_hbm, shift_hbm, scale_hbm, gate_hbm, wqkv_hbm, wp_hbm, wcq_hbm, wcp_hbm, ckv_hbm, te_hbm,
    out_ref,
    x_ref, shift_ref, scale_ref, gate_ref, ckv_ref, te_ref, wqkv, wp, wp_far, wcq, wcp, wcp_far,
    s1, t32, msg, xin, normed, qkv, att, att_far, branch, o2, om, o1,
    te_pad, part, core_in, part_x, x_in, part_z, z_in, part_y, y_in, full, tk, tv,
    load_sem, w_send, w_recv, s1_send, s1_recv, s2_send, s2_recv,
    a_send, a_recv, o2_send, o2_recv, o1_send, o1_recv,
    c_send, c_recv, x_send, x_recv, z_send, z_recv, y_send, y_recv,
):
    seq, hi = lax.axis_index("seq"), lax.axis_index("tp")
    z, q = seq // NQ, lax.rem(seq, NQ)
    core, spot = lax.rem(q, 2), q // 2

    def other_y(index):
        return index + 2 - 4 * lax.rem(index // 2, 2)

    def group_of(index):
        return index + hi * (other_y(index) - index)

    def place_of(index):
        group = group_of(index)
        return lax.rem(group, 2) * 8 + group // 2

    def at_z(index):
        return (index * NQ + q, hi)

    def at_q(index):
        return (z * NQ + index, hi)

    def at_x(index):
        return at_q(index * 4 + lax.rem(q, 4))

    x = q // 4
    pair = (z * NQ + other_y(q), 1 - hi)
    sibling = at_q(q + 1 - 2 * core)

    loads = [
        pltpu.make_async_copy(source, target, load_sem.at[n])
        for n, (source, target) in enumerate(
            (
                (wqkv_hbm, wqkv), (wp_hbm, wp), (wcq_hbm, wcq), (wcp_hbm, wcp), (x_hbm, x_ref),
                (shift_hbm, shift_ref), (scale_hbm, scale_ref), (gate_hbm, gate_ref), (ckv_hbm, ckv_ref), (te_hbm, te_ref),
            )
        )
    ]
    for load in loads:
        load.start()

    barrier = pltpu.get_barrier_semaphore()
    for step in range(1, NZ):
        pl.semaphore_signal(barrier, inc=1, device_id=at_z(lax.rem(z + step, NZ)), device_id_type=MESH)
    for step in range(1, NQ):
        pl.semaphore_signal(barrier, inc=1, device_id=at_q(lax.rem(q + step, NQ)), device_id_type=MESH)
    pl.semaphore_signal(barrier, inc=1, device_id=pair, device_id_type=MESH)
    pl.semaphore_wait(barrier, NZ - 1 + NQ - 1 + 1)

    def remote(source, target, send, recv, device):
        return pltpu.make_async_remote_copy(
            src_ref=source, dst_ref=target, send_sem=send, recv_sem=recv, device_id=device, device_id_type=MESH
        )

    sent = []

    def send(source, target, send_sem, recv_sem, device, when=None):
        copy = remote(source, target, send_sem, recv_sem, device)
        if when is None:
            copy.start()
        else:
            pl.when(when)(copy.start)
        sent.append((copy, when))

    def arrived(target, recv_sem, device, when=None):
        copy = remote(target, target, c_send.at[0], recv_sem, device)
        if when is None:
            copy.wait_recv()
        else:
            pl.when(when)(copy.wait_recv)

    def drain():
        for copy, when in sent:
            if when is None:
                copy.wait_send()
            else:
                pl.when(when)(copy.wait_send)
        sent.clear()

    def text_products():
        loads[8].wait()
        loads[9].wait()
        te_pad[...] = jnp.zeros_like(te_pad)
        te_pad[:, :TEXT_LEN] = te_ref[...]
        part[190:] = jnp.zeros((2, 16, 128), jnp.bfloat16)
        for which in range(2):
            product = lax.dot_general(
                te_pad[:, :TEXT_ROWS], ckv_ref[which], (((0,), (0,)), ((), ())), preferred_element_type=jnp.float32
            ).astype(jnp.bfloat16)
            product = jnp.concatenate([product, jnp.zeros((TEXT_ROWS, 64), jnp.bfloat16)], axis=1)
            for r in range(TEXT_ROWS // 16):
                for tile in range(5):
                    part[r * 10 + which * 5 + tile] = product[r * 16 : r * 16 + 16, tile * 128 : tile * 128 + 128]
        send(part.at[pl.ds(96 - 96 * core, 96)], core_in, c_send.at[0], c_recv.at[0], sibling)

    def text_core_sum():
        arrived(core_in, c_recv.at[0], sibling)
        part_x[...] = (part[pl.ds(96 * core, 96)].astype(jnp.float32) + core_in[...].astype(jnp.float32)).astype(jnp.bfloat16)
        for step in range(1, 4):
            target = lax.rem(x + step, 4)
            send(part_x.at[pl.ds(24 * target, 24)], x_in.at[x], x_send.at[0, step], x_recv.at[0, x], at_x(target))

    def text_x_sum():
        total = part_x[pl.ds(24 * x, 24)].astype(jnp.float32)
        for step in range(1, 4):
            source = lax.rem(x + step, 4)
            arrived(x_in.at[source], x_recv.at[0, source], at_x(source))
            total += x_in[source].astype(jnp.float32)
        part_z[...] = total.astype(jnp.bfloat16)
        for step in range(1, NZ):
            target = lax.rem(z + step, NZ)
            send(part_z.at[pl.ds(3 * target, 3)], z_in.at[z], z_send.at[0, step], z_recv.at[0, z], at_z(target))

    def text_z_sum():
        total = part_z[pl.ds(3 * z, 3)].astype(jnp.float32)
        for step in range(1, NZ):
            source = lax.rem(z + step, NZ)
            arrived(z_in.at[source], z_recv.at[0, source], at_z(source))
            total += z_in[source].astype(jnp.float32)
        part_y[...] = total.astype(jnp.bfloat16)
        send(part_y, y_in, y_send.at[0], y_recv.at[0], at_q(other_y(q)))

    def text_y_sum():
        arrived(y_in, y_recv.at[0], at_q(other_y(q)))
        mine = full.at[pl.ds(96 * core + 24 * x + 3 * z, 3)]
        mine[...] = (part_y[...].astype(jnp.float32) + y_in[...].astype(jnp.float32)).astype(jnp.bfloat16)
        for step in range(1, NZ):
            send(mine, mine, z_send.at[1, step], z_recv.at[1, z], at_z(lax.rem(z + step, NZ)))

    def text_z_gather():
        for step in range(1, NZ):
            source = lax.rem(z + step, NZ)
            arrived(full.at[pl.ds(96 * core + 24 * x + 3 * source, 3)], z_recv.at[1, source], at_z(source))
        mine = full.at[pl.ds(96 * core + 24 * x, 24)]
        for step in range(1, 4):
            send(mine, mine, x_send.at[1, step], x_recv.at[1, x], at_x(lax.rem(x + step, 4)))

    def text_x_gather():
        for step in range(1, 4):
            source = lax.rem(x + step, 4)
            arrived(full.at[pl.ds(96 * core + 24 * source, 24)], x_recv.at[1, source], at_x(source))
        mine = full.at[pl.ds(96 * core, 96)]
        send(mine, mine, c_send.at[1], c_recv.at[1], sibling)

    def text_core_gather():
        arrived(full.at[pl.ds(96 - 96 * core, 96)], c_recv.at[1], sibling)
        for which, target in enumerate((tk, tv)):
            for r in range(TEXT_ROWS // 16):
                for tile in range(5):
                    width = min(128, WIDTH - tile * 128)
                    target[r * 16 : r * 16 + 16, tile * 128 : tile * 128 + width] = full[r * 10 + which * 5 + tile][:, :width]

    for half in range(2):
        for n, step in enumerate((4, 3, 5, 2, 6, 1, 7)):
            target = lax.rem(z + step, NZ)
            send(
                x_hbm.at[pl.ds(pl.multiple_of(target * 32 + half * 16, 16), 16)],
                s1.at[z, half], s1_send.at[n, half], s1_recv.at[z, half], at_z(target),
            )
    half_rows = pl.ds(pl.multiple_of(core * 288, 288), 288)
    for n, (source, target) in enumerate(((wp_hbm, wp_far), (wcp_hbm, wcp_far))):
        send(source.at[half_rows], target.at[half_rows], w_send.at[n], w_recv.at[n], pair)
    loads[4].wait()
    for half in range(2):
        s1[z, half] = x_ref[pl.ds(pl.multiple_of(z * 32 + half * 16, 16), 16)]
    text_products()

    for half in range(2):
        for step in range(1, NZ):
            source = lax.rem(z + step, NZ)
            arrived(s1.at[source, half], s1_recv.at[source, half], at_z(source))
        def spread_in(tile, carry):
            lanes = pl.ds(pl.multiple_of(tile * 128, 128), 128)
            for n in range(NZ):
                t32[n * 16 : (n + 1) * 16] = s1[n, half, :, lanes].astype(jnp.float32)
            for n in range(8):
                first = t32[pl.ds(2 * n, 8, stride=16), :]
                second = t32[pl.ds(2 * n + 1, 8, stride=16), :]
                msg[half * 8 + n, :, lanes] = jnp.concatenate([first, second], axis=0).astype(jnp.bfloat16)
            return carry

        lax.fori_loop(0, D // 128, spread_in, 0)
        for step in range(8):
            dest = 2 * lax.rem(spot + step, 8) + half
            when = None if step else core != half
            send(msg.at[place_of(dest)], xin.at[q], s2_send.at[half * 8 + step], s2_recv.at[q], at_q(dest), when)
        if half:
            text_x_sum()
        else:
            text_core_sum()
    xin[q] = msg[place_of(q)]
    for step in range(1, NQ):
        source = lax.rem(q + step, NQ)
        arrived(xin.at[source], s2_recv.at[source], at_q(source))

    for n in (5, 6, 7):
        loads[n].wait()

    def norm_rows(n, carry):
        values = xin[n].astype(jnp.float32)
        center = jnp.mean(values, axis=-1, keepdims=True)
        values = values - center
        spread = jnp.mean(jnp.square(values), axis=-1, keepdims=True)
        values = values * lax.rsqrt(spread + 1e-06) * (1.0 + scale_ref[...].reshape(1, D)) + shift_ref[...].reshape(1, D)
        normed[rows_of(n, 16)] = values.astype(jnp.bfloat16)
        return carry

    lax.fori_loop(0, NQ, norm_rows, 0)
    loads[0].wait()

    def project(n, carry):
        qkv[n] = across(normed[...], wqkv[n])
        return carry

    lax.fori_loop(0, 3, project, 0)

    text_z_sum()

    for n, target in enumerate((wp_far, wcp_far)):
        arrived(target.at[half_rows], w_recv.at[n], pair)
        send(target.at[half_rows], target.at[half_rows], w_send.at[2 + n], w_recv.at[2 + n], sibling)

    row = lax.broadcasted_iota(jnp.int32, (TOKENS, TOKENS), 0)
    column = lax.broadcasted_iota(jnp.int32, (TOKENS, TOKENS), 1)
    same = lax.rem(row // 8, 2) == lax.rem(column // 8, 2)

    def put(target):
        def store(tile, piece):
            target[:, tile * 128 : tile * 128 + piece.shape[1]] = piece

        return store

    attend(qkv.at[0], qkv.at[1], qkv.at[2], same, put(att.at[0]))
    send(att.at[0], att_far.at[0], a_send.at[0], a_recv.at[0], pair)
    text_y_sum()
    loads[1].wait()
    branch[...] = jnp.dot(att[0], wp[...], preferred_element_type=jnp.float32)
    other_rows = pl.ds(pl.multiple_of(288 - core * 288, 288), 288)
    arrived(wp_far.at[other_rows], w_recv.at[2], sibling)
    text_z_gather()
    arrived(att_far.at[0], a_recv.at[0], pair)
    branch[...] = (branch[...] + jnp.dot(att_far[0], wp_far[...], preferred_element_type=jnp.float32)) * gate_ref[...].reshape(1, D)

    def mix_rows(n, carry):
        rows = rows_of(n, 16)
        normed[rows] = (xin[n].astype(jnp.float32) + branch[rows]).astype(jnp.bfloat16)
        return carry

    lax.fori_loop(0, NQ, mix_rows, 0)
    text_x_gather()
    loads[2].wait()
    qkv[0] = across(normed[...], wcq[...])
    text_core_gather()
    text = lax.broadcasted_iota(jnp.int32, (1, TEXT_ROWS), 1)
    attend(qkv.at[0], tk, tv, text < length_ref[0], put(att.at[1]))
    send(att.at[1], att_far.at[1], a_send.at[1], a_recv.at[1], pair)
    loads[3].wait()
    branch[...] += jnp.dot(att[1], wcp[...], preferred_element_type=jnp.float32)
    arrived(wcp_far.at[other_rows], w_recv.at[3], sibling)
    arrived(att_far.at[1], a_recv.at[1], pair)
    branch[...] += jnp.dot(att_far[1], wcp_far[...], preferred_element_type=jnp.float32)

    drain()

    for n in range(NQ):
        om[n] = branch[n * 16 : (n + 1) * 16].astype(jnp.bfloat16)
    place = place_of(q)
    for step in range(1, NQ):
        dest = lax.rem(q + step, NQ)
        send(om.at[dest], o2.at[place], o2_send.at[step], o2_recv.at[place], at_q(dest))
    o2[place] = om[q]
    for half in range(2):
        for step in range(8):
            source = 2 * lax.rem(spot + step, 8) + half
            slot = place_of(source)
            arrived(o2.at[slot], o2_recv.at[slot], at_q(source), None if step else core != half)
        def spread_out(tile, carry):
            lanes = pl.ds(pl.multiple_of(tile * 128, 128), 128)
            for n in range(8):
                t32[n * 16 : (n + 1) * 16] = o2[half * 8 + n, :, lanes].astype(jnp.float32)
            for n in range(NZ):
                msg[2 * n + half, :, lanes] = t32[pl.ds(n, 16, stride=8), :].astype(jnp.bfloat16)
            return carry

        lax.fori_loop(0, D // 128, spread_out, 0)
        for n, step in enumerate((4, 3, 5, 2, 6, 1, 7)):
            target = lax.rem(z + step, NZ)
            send(
                msg.at[2 * target + half], o1.at[2 * z + half], o1_send.at[n, half], o1_recv.at[z, half], at_z(target)
            )
        o1[2 * z + half] = msg[2 * z + half]
    for half in range(2):
        for step in range(1, NZ):
            source = lax.rem(z + step, NZ)
            arrived(o1.at[2 * source + half], o1_recv.at[source, half], at_z(source))

    def finish(n, carry):
        rows = rows_of(n, 16)
        out_ref[rows] = x_ref[rows].astype(jnp.float32) + o1[n].astype(jnp.float32)
        return carry

    lax.fori_loop(0, NQ, finish, 0)
    drain()


def mega(length, x, shift, scale, gate, wqkv, wp, wcq, wcp, ckv, te):
    vmem = pl.BlockSpec(memory_space=pltpu.VMEM)
    hbm = pl.BlockSpec(memory_space=pltpu.HBM)
    bf16, f32 = jnp.bfloat16, jnp.float32
    dma = pltpu.SemaphoreType.DMA
    return pl.pallas_call(
        kernel,
        out_shape=jax.ShapeDtypeStruct((TOKENS, D), f32),
        in_specs=[pl.BlockSpec(memory_space=pltpu.SMEM)] + [hbm] * 10,
        out_specs=vmem,
        scratch_shapes=[
            pltpu.VMEM((TOKENS, D), bf16),
            pltpu.VMEM((D,), f32),
            pltpu.VMEM((D,), f32),
            pltpu.VMEM((D,), f32),
            pltpu.VMEM((2, 32, WIDTH), bf16),
            pltpu.VMEM((32, TEXT_LEN), bf16),
            pltpu.VMEM((3, WIDTH, D), bf16),
            pltpu.VMEM((WIDTH, D), bf16),
            pltpu.VMEM((WIDTH, D), bf16),
            pltpu.VMEM((WIDTH, D), bf16),
            pltpu.VMEM((WIDTH, D), bf16),
            pltpu.VMEM((WIDTH, D), bf16),
            pltpu.VMEM((NZ, 2, 16, D), bf16),
            pltpu.VMEM((128, 128), f32),
            pltpu.VMEM((16, 16, D), bf16),
            pltpu.VMEM((16, 16, D), bf16),
            pltpu.VMEM((TOKENS, D), bf16),
            pltpu.VMEM((3, TOKENS, WIDTH), bf16),
            pltpu.VMEM((2, TOKENS, WIDTH), bf16),
            pltpu.VMEM((2, TOKENS, WIDTH), bf16),
            pltpu.VMEM((TOKENS, D), f32),
            pltpu.VMEM((16, 16, D), bf16),
            pltpu.VMEM((16, 16, D), bf16),
            pltpu.VMEM((16, 16, D), bf16),
            pltpu.VMEM((32, 384), bf16),
            pltpu.VMEM((192, 16, 128), bf16),
            pltpu.VMEM((96, 16, 128), bf16),
            pltpu.VMEM((96, 16, 128), bf16),
            pltpu.VMEM((4, 24, 16, 128), bf16),
            pltpu.VMEM((24, 16, 128), bf16),
            pltpu.VMEM((8, 3, 16, 128), bf16),
            pltpu.VMEM((3, 16, 128), bf16),
            pltpu.VMEM((3, 16, 128), bf16),
            pltpu.VMEM((192, 16, 128), bf16),
            pltpu.VMEM((TEXT_ROWS, WIDTH), bf16),
            pltpu.VMEM((TEXT_ROWS, WIDTH), bf16),
            dma((10,)), dma((4,)), dma((4,)),
            dma((7, 2)), dma((8, 2)), dma((16,)), dma((16,)),
            dma((2,)), dma((2,)), dma((16,)), dma((16,)), dma((7, 2)), dma((8, 2)),
            dma((2,)), dma((2,)), dma((2, 4)), dma((2, 4)), dma((2, 8)), dma((2, 8)), dma((1,)), dma((1,)),
        ],
        compiler_params=pltpu.CompilerParams(
            collective_id=0, has_side_effects=True, vmem_limit_bytes=60 * 1024 * 1024
        ),
        cost_estimate=pl.CostEstimate(flops=4_000_000_000, bytes_accessed=12_000_000, transcendentals=2_000_000),
        name="stdit",
    )(length, x, shift, scale, gate, wqkv, wp, wcq, wcp, ckv, te)


def body(
    video_latent, shift_temporal, scale_temporal, gate_temporal, temporal_qkv, temporal_proj,
    cross_query, cross_kv, cross_proj, text_embed, text_length,
):
    out = mega(
        text_length, video_latent.reshape(TOKENS, D),
        shift_temporal, scale_temporal, gate_temporal,
        jnp.transpose(temporal_qkv, (1, 2, 0)), temporal_proj, cross_query.T, cross_proj, cross_kv, text_embed.T,
    )
    return out.reshape(1, TOKENS, D)


def solution(mesh):
    return jax.shard_map(
        body,
        mesh=mesh,
        in_specs=(
            P("seq", None, None), P(), P(), P(), P(None, None, "tp"), P("tp", None), P(None, "tp"),
            P(None, "seq", "tp"), P("tp", None), P(None, "seq"), P(),
        ),
        out_specs=P("seq", None, None),
        check_vma=False,
    )
```

```python
import jax
import jax.numpy as jnp
from jax import lax
from jax.experimental import pallas as pl
from jax.experimental.pallas import tpu as pltpu
from jax.sharding import PartitionSpec as P

D = 1152
HD = 72
HEADS = 8
WIDTH = HEADS * HD
TOKENS = 256
FRAMES = 128
LOW, HIGH = 640, 512
NZ = 8
NQ = 16
TEXT_LEN = 300
TEXT_ROWS = 304
EXP_SCALE = HD ** (-0.5) * 1.4426950408889634
MESH = pl.DeviceIdType.MESH


def rows_of(index, size):
    return pl.ds(pl.multiple_of(index * size, size), size)


def attend(query, key, value, visible, store):
    tiles = [None] * 5
    for head in range(HEADS):
        low, high = head * HD, (head + 1) * HD
        first, last = low // 128, (high - 1) // 128
        start, end = first * 128, min((last + 1) * 128, WIDTH)
        rows = query[:, start:end]
        lane = lax.broadcasted_iota(jnp.int32, rows.shape, 1) + start
        rows = jnp.where((lane >= low) & (lane < high), rows, jnp.zeros_like(rows))
        scores = lax.dot_general(
            rows, key[:, start:end], (((1,), (1,)), ((), ())), preferred_element_type=jnp.float32
        )
        if visible is not None:
            scores = jnp.where(visible, scores, -1e30)
        top = jnp.max(scores, axis=-1, keepdims=True)
        weights = jnp.exp2((scores - top) * EXP_SCALE)
        total = jnp.sum(weights, axis=-1, keepdims=True)
        mixed = jnp.dot(
            weights.astype(jnp.bfloat16), value[:, start:end], preferred_element_type=jnp.float32
        ) * (1.0 / total)
        for tile in range(first, last + 1):
            piece = mixed[:, tile * 128 - start : min((tile + 1) * 128, WIDTH) - start]
            if tiles[tile] is not None:
                lane = lax.broadcasted_iota(jnp.int32, piece.shape, 1) + tile * 128
                piece = jnp.where(lane >= low, piece, tiles[tile])
            tiles[tile] = piece
            if high >= min((tile + 1) * 128, WIDTH):
                store(tile, piece.astype(jnp.bfloat16))


def across(rows, weights):
    return lax.dot_general(
        rows, weights, (((1,), (1,)), ((), ())), preferred_element_type=jnp.float32
    ).astype(jnp.bfloat16)


def kernel(
    length_ref, x_hbm, shift_hbm, scale_hbm, gate_hbm, wqkv_hbm, wp_hbm, wcq_hbm, wcp_hbm, ckv_hbm, te_hbm,
    out_hbm,
    shift_ref, scale_ref, gate_ref, ckv_ref, te_ref, wqkv, wp, wp_far, wcq, wcp, wcp_far,
    s1, t32, u32, v32, msg, xin, normed, qkv, att, att_far, branch, om, o2, back,
    te_pad, part, core_in, part_x, x_in, part_z, z_in, part_y, y_in, full, tk, tv,
    load_sem, w_send, w_recv, s1_send, s1_recv, s2_send, s2_recv,
    a_send, a_recv, o2_send, o2_recv, o1_send, o1_recv,
    c_send, c_recv, x_send, x_recv, z_send, z_recv, y_send, y_recv, own_sem,
):
    seq, hi = lax.axis_index("seq"), lax.axis_index("tp")
    z, q = seq // NQ, lax.rem(seq, NQ)
    core, spot = lax.rem(q, 2), q // 2

    def other_y(index):
        return index + 2 - 4 * lax.rem(index // 2, 2)

    def group_of(index):
        return index + hi * (other_y(index) - index)

    def place_of(index):
        group = group_of(index)
        return lax.rem(group, 2) * 8 + group // 2

    def at_z(index):
        return (index * NQ + q, hi)

    def at_q(index):
        return (z * NQ + index, hi)

    def at_x(index):
        return at_q(index * 4 + lax.rem(q, 4))

    x = q // 4
    pair = (z * NQ + other_y(q), 1 - hi)
    sibling = at_q(q + 1 - 2 * core)

    loads = [
        pltpu.make_async_copy(source, target, load_sem.at[n])
        for n, (source, target) in enumerate(
            (
                (te_hbm, te_ref), (ckv_hbm, ckv_ref), (shift_hbm, shift_ref), (scale_hbm, scale_ref),
                (gate_hbm, gate_ref), (wqkv_hbm, wqkv), (wp_hbm, wp), (wcq_hbm, wcq), (wcp_hbm, wcp),
            )
        )
    ]
    for load in loads:
        load.start()

    barrier = pltpu.get_barrier_semaphore()
    for step in range(1, NZ):
        pl.semaphore_signal(barrier, inc=1, device_id=at_z(lax.rem(z + step, NZ)), device_id_type=MESH)
    for step in range(1, NQ):
        pl.semaphore_signal(barrier, inc=1, device_id=at_q(lax.rem(q + step, NQ)), device_id_type=MESH)
    pl.semaphore_signal(barrier, inc=1, device_id=pair, device_id_type=MESH)

    def remote(source, target, send, recv, device):
        return pltpu.make_async_remote_copy(
            src_ref=source, dst_ref=target, send_sem=send, recv_sem=recv, device_id=device, device_id_type=MESH
        )

    sent = []

    def send(source, target, send_sem, recv_sem, device, when=None):
        copy = remote(source, target, send_sem, recv_sem, device)
        if when is None:
            copy.start()
        else:
            pl.when(when)(copy.start)
        sent.append((copy, when))

    def arrived(target, recv_sem, device, when=None):
        copy = remote(target, target, c_send.at[0], recv_sem, device)
        if when is None:
            copy.wait_recv()
        else:
            pl.when(when)(copy.wait_recv)

    def drain():
        for copy, when in sent:
            if when is None:
                copy.wait_send()
            else:
                pl.when(when)(copy.wait_send)
        sent.clear()

    def text_products():
        loads[0].wait()
        loads[1].wait()
        te_pad[...] = jnp.zeros_like(te_pad)
        te_pad[:, :TEXT_LEN] = te_ref[...]
        part[190:] = jnp.zeros((2, 16, 128), jnp.bfloat16)
        for which in range(2):
            product = lax.dot_general(
                te_pad[:, :TEXT_ROWS], ckv_ref[which], (((0,), (0,)), ((), ())), preferred_element_type=jnp.float32
            ).astype(jnp.bfloat16)
            product = jnp.concatenate([product, jnp.zeros((TEXT_ROWS, 64), jnp.bfloat16)], axis=1)
            for r in range(TEXT_ROWS // 16):
                for tile in range(5):
                    part[r * 10 + which * 5 + tile] = product[r * 16 : r * 16 + 16, tile * 128 : tile * 128 + 128]

    def text_send():
        send(part.at[pl.ds(96 - 96 * core, 96)], core_in, c_send.at[0], c_recv.at[0], sibling)

    def text_core_sum():
        arrived(core_in, c_recv.at[0], sibling)
        part_x[...] = (part[pl.ds(96 * core, 96)].astype(jnp.float32) + core_in[...].astype(jnp.float32)).astype(jnp.bfloat16)
        for step in range(1, 4):
            target = lax.rem(x + step, 4)
            send(part_x.at[pl.ds(24 * target, 24)], x_in.at[x], x_send.at[0, step], x_recv.at[0, x], at_x(target))

    def text_x_sum():
        total = part_x[pl.ds(24 * x, 24)].astype(jnp.float32)
        for step in range(1, 4):
            source = lax.rem(x + step, 4)
            arrived(x_in.at[source], x_recv.at[0, source], at_x(source))
            total += x_in[source].astype(jnp.float32)
        part_z[...] = total.astype(jnp.bfloat16)
        for step in range(1, NZ):
            target = lax.rem(z + step, NZ)
            send(part_z.at[pl.ds(3 * target, 3)], z_in.at[z], z_send.at[0, step], z_recv.at[0, z], at_z(target))

    def text_z_sum():
        total = part_z[pl.ds(3 * z, 3)].astype(jnp.float32)
        for step in range(1, NZ):
            source = lax.rem(z + step, NZ)
            arrived(z_in.at[source], z_recv.at[0, source], at_z(source))
            total += z_in[source].astype(jnp.float32)
        part_y[...] = total.astype(jnp.bfloat16)
        send(part_y, y_in, y_send.at[0], y_recv.at[0], at_q(other_y(q)))

    def text_y_sum():
        arrived(y_in, y_recv.at[0], at_q(other_y(q)))
        mine = full.at[pl.ds(96 * core + 24 * x + 3 * z, 3)]
        mine[...] = (part_y[...].astype(jnp.float32) + y_in[...].astype(jnp.float32)).astype(jnp.bfloat16)
        for step in range(1, NZ):
            send(mine, mine, z_send.at[1, step], z_recv.at[1, z], at_z(lax.rem(z + step, NZ)))

    def text_z_gather():
        for step in range(1, NZ):
            source = lax.rem(z + step, NZ)
            arrived(full.at[pl.ds(96 * core + 24 * x + 3 * source, 3)], z_recv.at[1, source], at_z(source))
        mine = full.at[pl.ds(96 * core + 24 * x, 24)]
        for step in range(1, 4):
            send(mine, mine, x_send.at[1, step], x_recv.at[1, x], at_x(lax.rem(x + step, 4)))

    def text_x_gather():
        for step in range(1, 4):
            source = lax.rem(x + step, 4)
            arrived(full.at[pl.ds(96 * core + 24 * source, 24)], x_recv.at[1, source], at_x(source))
        mine = full.at[pl.ds(96 * core, 96)]
        send(mine, mine, c_send.at[1], c_recv.at[1], sibling)

    def text_core_gather():
        arrived(full.at[pl.ds(96 - 96 * core, 96)], c_recv.at[1], sibling)
        for which, target in enumerate((tk, tv)):
            for r in range(TEXT_ROWS // 16):
                for tile in range(5):
                    width = min(128, WIDTH - tile * 128)
                    target[r * 16 : r * 16 + 16, tile * 128 : tile * 128 + width] = full[r * 10 + which * 5 + tile][:, :width]

    half_rows = pl.ds(pl.multiple_of(core * 288, 288), 288)
    other_rows = pl.ds(pl.multiple_of(288 - core * 288, 288), 288)
    own = []

    def location_rows(index, stream):
        return pl.ds(pl.multiple_of(index * 32 + stream * 16, 16), 16)

    def in1_send(stream):
        for n, step in enumerate((4, 3, 5, 2, 6, 1, 7)):
            target = lax.rem(z + step, NZ)
            send(
                x_hbm.at[location_rows(target, stream)],
                s1.at[z, stream], s1_send.at[n, stream], s1_recv.at[z, stream], at_z(target),
            )
        copy = pltpu.make_async_copy(x_hbm.at[location_rows(z, stream)], s1.at[z, stream], own_sem.at[stream])
        copy.start()
        own.append(copy)

    def in1_done(stream):
        own[stream].wait()
        for step in range(1, NZ):
            source = lax.rem(z + step, NZ)
            arrived(s1.at[source, stream], s1_recv.at[source, stream], at_z(source))

    def in2_send(stream):
        def spread_in(tile, carry):
            lanes = pl.ds(pl.multiple_of(tile * 128, 128), 128)
            upper = pl.ds(pl.multiple_of(lax.rem(tile + 5, 9) * 128, 128), 128)
            for n in range(NZ):
                t32[n * 16 : (n + 1) * 16] = s1[n, stream, :, lanes].astype(jnp.float32)
                u32[n * 16 : (n + 1) * 16] = s1[n, stream, :, upper].astype(jnp.float32)
            for n in range(NQ):
                both = jnp.concatenate([t32[pl.ds(n, 8, stride=16), :], u32[pl.ds(n, 8, stride=16), :]], axis=0)
                msg[stream, n, :, lanes] = both.astype(jnp.bfloat16)
            return carry

        lax.fori_loop(0, 5, spread_in, 0)
        for step in (8, 4, 12, 10, 6, 14, 2, 9, 5, 13, 11, 7, 15, 3, 1):
            dest = lax.rem(q + step, NQ)
            send(msg.at[stream, place_of(dest)], xin.at[stream, q], s2_send.at[stream, step], s2_recv.at[stream, q], at_q(dest))
        xin[stream, q] = msg[stream, place_of(q)]

    def in2_done(stream):
        for step in range(1, NQ):
            source = lax.rem(q + step, NQ)
            arrived(xin.at[stream, source], s2_recv.at[stream, source], at_q(source))

    def latent_rows(stream, n):
        first, second = xin[stream, 2 * n].astype(jnp.float32), xin[stream, 2 * n + 1].astype(jnp.float32)
        low = jnp.concatenate([first[:8], second[:8]], axis=0)
        high = jnp.concatenate([first[8:, :HIGH], second[8:, :HIGH]], axis=0)
        return jnp.concatenate([low, high], axis=1)

    def temporal_norm(stream):
        def norm_rows(n, carry):
            values = latent_rows(stream, n)
            center = jnp.mean(values, axis=-1, keepdims=True)
            values = values - center
            spread = jnp.mean(jnp.square(values), axis=-1, keepdims=True)
            values = values * lax.rsqrt(spread + 1e-06) * (1.0 + scale_ref[...].reshape(1, D)) + shift_ref[...].reshape(1, D)
            normed[rows_of(n, 16)] = values.astype(jnp.bfloat16)
            return carry

        lax.fori_loop(0, 8, norm_rows, 0, unroll=2)

    def temporal(stream):
        def project(n, carry):
            qkv[n] = across(normed[...], wqkv[n])
            return carry

        lax.fori_loop(0, 3, project, 0)
        attend(qkv.at[0], qkv.at[1], qkv.at[2], None, put(att.at[0, stream]))
        swap(0, stream)

    def put(target):
        def store(tile, piece):
            target[:, tile * 128 : tile * 128 + piece.shape[1]] = piece

        return store

    def swap(kind, stream):
        send(att.at[kind, stream], att_far.at[kind, stream], a_send.at[kind, stream], a_recv.at[kind, stream], pair)

    def swapped(kind, stream):
        arrived(att_far.at[kind, stream], a_recv.at[kind, stream], pair)

    def mix(stream):
        branch[stream] = jnp.dot(att[0, stream], wp[...], preferred_element_type=jnp.float32)
        swapped(0, stream)
        total = branch[stream] + jnp.dot(att_far[0, stream], wp_far[...], preferred_element_type=jnp.float32)
        branch[stream] = total * gate_ref[...].reshape(1, D)

        def mix_rows(n, carry):
            rows = rows_of(n, 16)
            normed[rows] = (latent_rows(stream, n) + branch[stream, rows]).astype(jnp.bfloat16)
            return carry

        lax.fori_loop(0, 8, mix_rows, 0)
        qkv[0] = across(normed[...], wcq[...])

    def cross(stream):
        text = lax.broadcasted_iota(jnp.int32, (1, TEXT_ROWS), 1)
        attend(qkv.at[0], tk, tv, text < length_ref[0], put(att.at[1, stream]))
        swap(1, stream)
        branch[stream] += jnp.dot(att[1, stream], wcp[...], preferred_element_type=jnp.float32)

    def out2_send(stream):
        branch[stream] += jnp.dot(att_far[1, stream], wcp_far[...], preferred_element_type=jnp.float32)

        def fold(n, carry):
            rows = branch[stream, rows_of(n, 8)]
            high = jnp.concatenate([rows[:, LOW:], jnp.zeros((8, LOW - HIGH), jnp.float32)], axis=1)
            om[stream, n] = jnp.concatenate([rows[:, :LOW], high], axis=0).astype(jnp.bfloat16)
            return carry

        lax.fori_loop(0, NQ, fold, 0, unroll=2)
        place = place_of(q)
        for step in (8, 4, 12, 10, 6, 14, 2, 9, 5, 13, 11, 7, 15, 3, 1):
            dest = lax.rem(q + step, NQ)
            send(om.at[stream, dest], o2.at[stream, place], o2_send.at[stream, step], o2_recv.at[stream, place], at_q(dest))
        o2[stream, place] = om[stream, q]

    def out1_send(stream):
        for step in range(1, NQ):
            source = lax.rem(q + step, NQ)
            arrived(o2.at[stream, place_of(source)], o2_recv.at[stream, place_of(source)], at_q(source))

        def spread_out(tile, carry):
            lanes = pl.ds(pl.multiple_of(tile * 128, 128), 128)
            for n in range(NQ):
                v32[n * 16 : (n + 1) * 16] = o2[stream, n, :, lanes].astype(jnp.float32)
            for n in range(NZ):
                back[stream, n, :, lanes] = v32[pl.ds(n, 16, stride=16), :].astype(jnp.bfloat16)

            @pl.when(tile < 4)
            def _():
                upper = pl.ds(pl.multiple_of(tile * 128 + LOW, 128), 128)
                for n in range(NZ):
                    back[stream, n, :, upper] = v32[pl.ds(n + 8, 16, stride=16), :].astype(jnp.bfloat16)

            return carry

        lax.fori_loop(0, 5, spread_out, 0)
        for n, step in enumerate((4, 3, 5, 2, 6, 1, 7)):
            target = lax.rem(z + step, NZ)
            send(
                back.at[stream, target], out_hbm.at[location_rows(z, stream)],
                o1_send.at[n, stream], o1_recv.at[z, stream], at_z(target),
            )
        copy = pltpu.make_async_copy(back.at[stream, z], out_hbm.at[location_rows(z, stream)], own_sem.at[2 + stream])
        copy.start()
        own.append(copy)

    def out1_done(stream):
        own[2 + stream].wait()
        for step in range(1, NZ):
            source = lax.rem(z + step, NZ)
            arrived(out_hbm.at[location_rows(source, stream)], o1_recv.at[source, stream], at_z(source))

    def far_weights(n, source, target):
        send(source.at[half_rows], target.at[half_rows], w_send.at[n], w_recv.at[n], pair)

    def forward_weights(n, target):
        arrived(target.at[half_rows], w_recv.at[n], pair)
        send(target.at[half_rows], target.at[half_rows], w_send.at[2 + n], w_recv.at[2 + n], sibling)

    text_products()
    pl.semaphore_wait(barrier, NZ - 1 + NQ - 1 + 1)
    in1_send(0)
    far_weights(0, wp_hbm, wp_far)
    in1_send(1)
    text_send()
    far_weights(1, wcp_hbm, wcp_far)
    in1_done(0)
    in2_send(0)
    text_core_sum()
    in1_done(1)
    in2_send(1)
    text_x_sum()
    for n in (2, 3, 4):
        loads[n].wait()
    in2_done(0)
    temporal_norm(0)
    text_z_sum()
    loads[5].wait()
    temporal(0)
    forward_weights(0, wp_far)
    text_y_sum()
    in2_done(1)
    temporal_norm(1)
    text_z_gather()
    temporal(1)
    text_x_gather()
    loads[6].wait()
    loads[7].wait()
    arrived(wp_far.at[other_rows], w_recv.at[2], sibling)
    mix(0)
    text_core_gather()
    loads[8].wait()
    cross(0)
    forward_weights(1, wcp_far)
    mix(1)
    cross(1)
    arrived(wcp_far.at[other_rows], w_recv.at[3], sibling)
    swapped(1, 0)
    out2_send(0)
    swapped(1, 1)
    out2_send(1)
    out1_send(0)
    out1_send(1)
    out1_done(0)
    out1_done(1)
    drain()


def mega(length, x, shift, scale, gate, wqkv, wp, wcq, wcp, ckv, te):
    bf16, f32 = jnp.bfloat16, jnp.float32
    dma, vmem = pltpu.SemaphoreType.DMA, pltpu.VMEM
    return pl.pallas_call(
        kernel,
        out_shape=jax.ShapeDtypeStruct((TOKENS, D), bf16),
        in_specs=[pl.BlockSpec(memory_space=pltpu.SMEM)] + [pl.BlockSpec(memory_space=pltpu.HBM)] * 10,
        out_specs=pl.BlockSpec(memory_space=pltpu.HBM),
        scratch_shapes=[
            vmem((D,), f32), vmem((D,), f32), vmem((D,), f32),
            vmem((2, 32, WIDTH), bf16), vmem((32, TEXT_LEN), bf16),
            vmem((3, WIDTH, D), bf16), vmem((WIDTH, D), bf16), vmem((WIDTH, D), bf16),
            vmem((WIDTH, D), bf16), vmem((WIDTH, D), bf16), vmem((WIDTH, D), bf16),
            vmem((NZ, 2, 16, D), bf16), vmem((128, 128), f32), vmem((128, 128), f32), vmem((256, 128), f32),
            vmem((2, NQ, 16, LOW), bf16), vmem((2, NQ, 16, LOW), bf16),
            vmem((FRAMES, D), bf16), vmem((3, FRAMES, WIDTH), bf16),
            vmem((2, 2, FRAMES, WIDTH), bf16), vmem((2, 2, FRAMES, WIDTH), bf16), vmem((2, FRAMES, D), f32),
            vmem((2, NQ, 16, LOW), bf16), vmem((2, NQ, 16, LOW), bf16), vmem((2, NZ, 16, D), bf16),
            vmem((32, 384), bf16), vmem((192, 16, 128), bf16), vmem((96, 16, 128), bf16), vmem((96, 16, 128), bf16),
            vmem((4, 24, 16, 128), bf16), vmem((24, 16, 128), bf16), vmem((8, 3, 16, 128), bf16),
            vmem((3, 16, 128), bf16), vmem((3, 16, 128), bf16), vmem((192, 16, 128), bf16),
            vmem((TEXT_ROWS, WIDTH), bf16), vmem((TEXT_ROWS, WIDTH), bf16),
            dma((9,)), dma((4,)), dma((4,)), dma((7, 2)), dma((8, 2)), dma((2, 16)), dma((2, 16)),
            dma((2, 2)), dma((2, 2)), dma((2, 16)), dma((2, 16)), dma((7, 2)), dma((8, 2)),
            dma((2,)), dma((2,)), dma((2, 4)), dma((2, 4)), dma((2, 8)), dma((2, 8)), dma((1,)), dma((1,)), dma((4,)),
        ],
        compiler_params=pltpu.CompilerParams(
            collective_id=0, has_side_effects=True, vmem_limit_bytes=60 * 1024 * 1024
        ),
        cost_estimate=pl.CostEstimate(flops=4_000_000_000, bytes_accessed=12_000_000, transcendentals=2_000_000),
        name="stdit",
    )(length, x, shift, scale, gate, wqkv, wp, wcq, wcp, ckv, te)


def body(
    video_latent, shift_temporal, scale_temporal, gate_temporal, temporal_qkv, temporal_proj,
    cross_query, cross_kv, cross_proj, text_embed, text_length,
):
    out = mega(
        text_length, video_latent.reshape(TOKENS, D),
        shift_temporal, scale_temporal, gate_temporal,
        jnp.transpose(temporal_qkv, (1, 2, 0)), temporal_proj, cross_query.T, cross_proj, cross_kv, text_embed.T,
    )
    return video_latent.astype(jnp.float32) + out.reshape(1, TOKENS, D).astype(jnp.float32)


def solution(mesh):
    return jax.shard_map(
        body,
        mesh=mesh,
        in_specs=(
            P("seq", None, None), P(), P(), P(), P(None, None, "tp"), P("tp", None), P(None, "tp"),
            P(None, "seq", "tp"), P("tp", None), P(None, "seq"), P(),
        ),
        out_specs=P("seq", None, None),
        check_vma=False,
    )
```

```python
import jax
import jax.numpy as jnp
from jax import lax
from jax.experimental import pallas as pl
from jax.experimental.pallas import tpu as pltpu
from jax.sharding import PartitionSpec as P

D = 1152
HD = 72
HEADS = 8
WIDTH = HEADS * HD
TOKENS = 256
FRAMES = 128
LOW, HIGH = 640, 512
NZ = 8
NQ = 16
TEXT_LEN = 300
TEXT_ROWS = 304
EXP_SCALE = HD ** (-0.5) * 1.4426950408889634
MESH = pl.DeviceIdType.MESH


def rows_of(index, size):
    return pl.ds(pl.multiple_of(index * size, size), size)


def dot(a, b, dims):
    return lax.dot_general(a, b, (dims, ((), ())), preferred_element_type=jnp.float32)


def attend(scores_of, value_of, visible, target):
    for group in range(0, HEADS, 4):
        scores = [scores_of(head) for head in range(group, group + 4)]
        weights, totals = [], []
        for score in scores:
            if visible is not None:
                score = jnp.where(visible, score, -1e30)
            top = jnp.max(score, axis=0, keepdims=True)
            weight = jnp.exp2((score - top) * EXP_SCALE)
            totals.append(1.0 / jnp.sum(weight, axis=0, keepdims=True))
            weights.append(weight.astype(jnp.bfloat16))
        mixed = [dot(value_of(group + n), weights[n], ((1,), (0,))) * totals[n] for n in range(4)]
        for n in (0, 2):
            target[(group + n) * HD : (group + n + 2) * HD] = jnp.concatenate(mixed[n : n + 2], axis=0).astype(jnp.bfloat16)


def kernel(
    length_ref, x_hbm, shift_hbm, scale_hbm, gate_hbm, wqkv_hbm, wp_hbm, wcq_hbm, wcp_hbm, ckv_hbm, te_hbm,
    out_hbm,
    shift_ref, scale_ref, gate_ref, ckv_ref, te_ref, wqkv, wp, wp_far, wcq, wcp,
    s1, t32, u32, v32, msg, xin, normed, qkv, att, att_far, branch, partial, give, taken, om, o2, back,
    te_pad, part, core_in, part_x, x_in, part_z, z_in, part_y, y_in, full, tk, tv,
    load_sem, w_send, w_recv, s1_send, s1_recv, s2_send, s2_recv,
    a_send, a_recv, o2_send, o2_recv, o1_send, o1_recv,
    c_send, c_recv, x_send, x_recv, z_send, z_recv, y_send, y_recv, own_sem,
):
    seq, hi = lax.axis_index("seq"), lax.axis_index("tp")
    z, q = seq // NQ, lax.rem(seq, NQ)
    core, spot = lax.rem(q, 2), q // 2

    def other_y(index):
        return index + 2 - 4 * lax.rem(index // 2, 2)

    def group_of(index):
        return index + hi * (other_y(index) - index)

    def place_of(index):
        group = group_of(index)
        return lax.rem(group, 2) * 8 + group // 2

    def at_z(index):
        return (index * NQ + q, hi)

    def at_q(index):
        return (z * NQ + index, hi)

    def at_x(index):
        return at_q(index * 4 + lax.rem(q, 4))

    x = q // 4
    pair = (z * NQ + other_y(q), 1 - hi)
    sibling = at_q(q + 1 - 2 * core)

    loads = [
        pltpu.make_async_copy(source, target, load_sem.at[n])
        for n, (source, target) in enumerate(
            (
                (te_hbm, te_ref), (ckv_hbm, ckv_ref), (shift_hbm, shift_ref), (scale_hbm, scale_ref),
                (gate_hbm, gate_ref), (wqkv_hbm, wqkv), (wp_hbm, wp), (wcq_hbm, wcq), (wcp_hbm, wcp),
            )
        )
    ]
    for load in loads:
        load.start()

    barrier = pltpu.get_barrier_semaphore()
    for step in range(1, NZ):
        pl.semaphore_signal(barrier, inc=1, device_id=at_z(lax.rem(z + step, NZ)), device_id_type=MESH)
    for step in range(1, NQ):
        pl.semaphore_signal(barrier, inc=1, device_id=at_q(lax.rem(q + step, NQ)), device_id_type=MESH)
    pl.semaphore_signal(barrier, inc=1, device_id=pair, device_id_type=MESH)

    def remote(source, target, send, recv, device):
        return pltpu.make_async_remote_copy(
            src_ref=source, dst_ref=target, send_sem=send, recv_sem=recv, device_id=device, device_id_type=MESH
        )

    sent = []

    def send(source, target, send_sem, recv_sem, device, when=None):
        copy = remote(source, target, send_sem, recv_sem, device)
        if when is None:
            copy.start()
        else:
            pl.when(when)(copy.start)
        sent.append((copy, when))

    def arrived(target, recv_sem, device, when=None):
        copy = remote(target, target, c_send.at[0], recv_sem, device)
        if when is None:
            copy.wait_recv()
        else:
            pl.when(when)(copy.wait_recv)

    def drain():
        for copy, when in sent:
            if when is None:
                copy.wait_send()
            else:
                pl.when(when)(copy.wait_send)
        sent.clear()

    def text_products():
        loads[0].wait()
        loads[1].wait()
        te_pad[...] = jnp.zeros_like(te_pad)
        te_pad[:, :TEXT_LEN] = te_ref[...]
        part[190:] = jnp.zeros((2, 16, 128), jnp.bfloat16)
        for which in range(2):
            product = lax.dot_general(
                te_pad[:, :TEXT_ROWS], ckv_ref[which], (((0,), (0,)), ((), ())), preferred_element_type=jnp.float32
            ).astype(jnp.bfloat16)
            product = jnp.concatenate([product, jnp.zeros((TEXT_ROWS, 64), jnp.bfloat16)], axis=1)
            for r in range(TEXT_ROWS // 16):
                for tile in range(5):
                    part[r * 10 + which * 5 + tile] = product[r * 16 : r * 16 + 16, tile * 128 : tile * 128 + 128]

    def text_send():
        send(part.at[pl.ds(96 - 96 * core, 96)], core_in, c_send.at[0], c_recv.at[0], sibling)

    def text_core_sum():
        arrived(core_in, c_recv.at[0], sibling)
        part_x[...] = (part[pl.ds(96 * core, 96)].astype(jnp.float32) + core_in[...].astype(jnp.float32)).astype(jnp.bfloat16)
        for step in range(1, 4):
            target = lax.rem(x + step, 4)
            send(part_x.at[pl.ds(24 * target, 24)], x_in.at[x], x_send.at[0, step], x_recv.at[0, x], at_x(target))

    def text_x_sum():
        total = part_x[pl.ds(24 * x, 24)].astype(jnp.float32)
        for step in range(1, 4):
            source = lax.rem(x + step, 4)
            arrived(x_in.at[source], x_recv.at[0, source], at_x(source))
            total += x_in[source].astype(jnp.float32)
        part_z[...] = total.astype(jnp.bfloat16)
        for step in range(1, NZ):
            target = lax.rem(z + step, NZ)
            send(part_z.at[pl.ds(3 * target, 3)], z_in.at[z], z_send.at[0, step], z_recv.at[0, z], at_z(target))

    def text_z_sum():
        total = part_z[pl.ds(3 * z, 3)].astype(jnp.float32)
        for step in range(1, NZ):
            source = lax.rem(z + step, NZ)
            arrived(z_in.at[source], z_recv.at[0, source], at_z(source))
            total += z_in[source].astype(jnp.float32)
        part_y[...] = total.astype(jnp.bfloat16)
        send(part_y, y_in, y_send.at[0], y_recv.at[0], at_q(other_y(q)))

    def text_y_sum():
        arrived(y_in, y_recv.at[0], at_q(other_y(q)))
        mine = full.at[pl.ds(96 * core + 24 * x + 3 * z, 3)]
        mine[...] = (part_y[...].astype(jnp.float32) + y_in[...].astype(jnp.float32)).astype(jnp.bfloat16)
        for step in range(1, NZ):
            send(mine, mine, z_send.at[1, step], z_recv.at[1, z], at_z(lax.rem(z + step, NZ)))

    def text_z_gather():
        for step in range(1, NZ):
            source = lax.rem(z + step, NZ)
            arrived(full.at[pl.ds(96 * core + 24 * x + 3 * source, 3)], z_recv.at[1, source], at_z(source))
        mine = full.at[pl.ds(96 * core + 24 * x, 24)]
        for step in range(1, 4):
            send(mine, mine, x_send.at[1, step], x_recv.at[1, x], at_x(lax.rem(x + step, 4)))

    def text_x_gather():
        for step in range(1, 4):
            source = lax.rem(x + step, 4)
            arrived(full.at[pl.ds(96 * core + 24 * source, 24)], x_recv.at[1, source], at_x(source))
        mine = full.at[pl.ds(96 * core, 96)]
        send(mine, mine, c_send.at[1], c_recv.at[1], sibling)

    def text_core_gather():
        arrived(full.at[pl.ds(96 - 96 * core, 96)], c_recv.at[1], sibling)
        for tile in range(5):
            width = min(128, WIDTH - tile * 128)
            rows = []
            for r in range(TEXT_ROWS // 16):
                tk[r * 16 : r * 16 + 16, tile * 128 : tile * 128 + width] = full[r * 10 + tile][:, :width]
                rows.append(full[r * 10 + 5 + tile].astype(jnp.float32))
            rows.append(jnp.zeros((384 - TEXT_ROWS, 128), jnp.float32))
            tv[tile * 128 : (tile + 1) * 128] = jnp.concatenate(rows, axis=0).T

    half_rows = pl.ds(pl.multiple_of(core * 288, 288), 288)
    other_rows = pl.ds(pl.multiple_of(288 - core * 288, 288), 288)
    own = []

    def location_rows(index, stream):
        return pl.ds(pl.multiple_of(index * 32 + stream * 16, 16), 16)

    def in1_send(stream):
        for n, step in enumerate((4, 3, 5, 2, 6, 1, 7)):
            target = lax.rem(z + step, NZ)
            send(
                x_hbm.at[location_rows(target, stream)],
                s1.at[z, stream], s1_send.at[n, stream], s1_recv.at[z, stream], at_z(target),
            )
        copy = pltpu.make_async_copy(x_hbm.at[location_rows(z, stream)], s1.at[z, stream], own_sem.at[stream])
        copy.start()
        own.append(copy)

    def in1_done(stream):
        own[stream].wait()
        for step in range(1, NZ):
            source = lax.rem(z + step, NZ)
            arrived(s1.at[source, stream], s1_recv.at[source, stream], at_z(source))

    def in2_send(stream):
        def spread_in(tile, carry):
            lanes = pl.ds(pl.multiple_of(tile * 128, 128), 128)
            upper = pl.ds(pl.multiple_of(lax.rem(tile + 5, 9) * 128, 128), 128)
            for n in range(NZ):
                t32[n * 16 : (n + 1) * 16] = s1[n, stream, :, lanes].astype(jnp.float32)
                u32[n * 16 : (n + 1) * 16] = s1[n, stream, :, upper].astype(jnp.float32)
            for n in range(NQ):
                both = jnp.concatenate([t32[pl.ds(n, 8, stride=16), :], u32[pl.ds(n, 8, stride=16), :]], axis=0)
                msg[stream, n, :, lanes] = both.astype(jnp.bfloat16)
            return carry

        lax.fori_loop(0, 5, spread_in, 0)
        for step in (8, 4, 12, 10, 6, 14, 2, 9, 5, 13, 11, 7, 15, 3, 1):
            dest = lax.rem(q + step, NQ)
            send(msg.at[stream, place_of(dest)], xin.at[stream, q], s2_send.at[stream, step], s2_recv.at[stream, q], at_q(dest))
        xin[stream, q] = msg[stream, place_of(q)]

    def in2_done(stream):
        for step in range(1, NQ):
            source = lax.rem(q + step, NQ)
            arrived(xin.at[stream, source], s2_recv.at[stream, source], at_q(source))

    def latent_rows(stream, n):
        first, second = xin[stream, 2 * n].astype(jnp.float32), xin[stream, 2 * n + 1].astype(jnp.float32)
        low = jnp.concatenate([first[:8], second[:8]], axis=0)
        high = jnp.concatenate([first[8:, :HIGH], second[8:, :HIGH]], axis=0)
        return jnp.concatenate([low, high], axis=1)

    def temporal_norm(stream):
        def norm_rows(n, carry):
            values = latent_rows(stream, n)
            center = jnp.mean(values, axis=-1, keepdims=True)
            values = values - center
            spread = jnp.mean(jnp.square(values), axis=-1, keepdims=True)
            values = values * lax.rsqrt(spread + 1e-06) * (1.0 + scale_ref[...].reshape(1, D)) + shift_ref[...].reshape(1, D)
            normed[rows_of(n, 16)] = values.astype(jnp.bfloat16)
            return carry

        lax.fori_loop(0, 8, norm_rows, 0, unroll=2)

    def head_rows(which, head):
        return qkv[which, head * HD : (head + 1) * HD].astype(jnp.bfloat16)

    def temporal(stream):
        def project(n, carry):
            qkv[n] = dot(wqkv[n], normed[...], ((1,), (1,)))
            return carry

        lax.fori_loop(0, 3, project, 0)
        attend(
            lambda head: dot(head_rows(1, head), head_rows(0, head), ((0,), (0,))),
            lambda head: head_rows(2, head), None, att.at[0, stream],
        )
        send(att.at[0, stream], att_far.at[stream], a_send.at[0, stream], a_recv.at[0, stream], pair)

    def mix(stream):
        branch[stream] = dot(att[0, stream], wp[...], ((0,), (0,)))
        arrived(att_far.at[stream], a_recv.at[0, stream], pair)
        total = branch[stream] + dot(att_far[stream], wp_far[...], ((0,), (0,)))
        branch[stream] = total * gate_ref[...].reshape(1, D)

        def mix_rows(n, carry):
            rows = rows_of(n, 16)
            normed[rows] = (latent_rows(stream, n) + branch[stream, rows]).astype(jnp.bfloat16)
            return carry

        lax.fori_loop(0, 8, mix_rows, 0, unroll=2)
        qkv[0] = dot(wcq[...], normed[...], ((1,), (1,)))

    def cross(stream):
        row = lax.broadcasted_iota(jnp.int32, (TEXT_ROWS, FRAMES), 0)

        def scores_of(head):
            low, high = head * HD, (head + 1) * HD
            start, end = low // 128 * 128, min(-(-high // 128) * 128, WIDTH)
            place = lax.broadcasted_iota(jnp.int32, (end - start, FRAMES), 0) + start
            query = jnp.where((place >= low) & (place < high), qkv[0, start:end], 0.0).astype(jnp.bfloat16)
            return dot(tk[:, start:end], query, ((1,), (0,)))

        def value_of(head):
            return tv[head * HD : (head + 1) * HD, :TEXT_ROWS].astype(jnp.bfloat16)

        attend(scores_of, value_of, row < length_ref[0], att.at[1, stream])
        partial[...] = dot(att[1, stream], wcp[...], ((0,), (0,)))

        def fold_partial(n, carry):
            give[stream, n] = fold(partial[rows_of(n, 8)]).astype(jnp.bfloat16)
            return carry

        lax.fori_loop(0, NQ, fold_partial, 0, unroll=2)
        send(give.at[stream], taken.at[stream], a_send.at[1, stream], a_recv.at[1, stream], pair)

    def fold(rows):
        high = jnp.concatenate([rows[:, LOW:], jnp.zeros((8, LOW - HIGH), jnp.float32)], axis=1)
        return jnp.concatenate([rows[:, :LOW], high], axis=0)

    def out2_add(stream):
        arrived(taken.at[stream], a_recv.at[1, stream], pair)

        def add_rows(n, carry):
            both = give[stream, n].astype(jnp.float32) + taken[stream, n].astype(jnp.float32)
            om[stream, n] = (fold(branch[stream, rows_of(n, 8)]) + both).astype(jnp.bfloat16)
            return carry

        lax.fori_loop(0, NQ, add_rows, 0, unroll=2)

    def out2_send(stream):
        place = place_of(q)
        for step in (8, 4, 12, 10, 6, 14, 2, 9, 5, 13, 11, 7, 15, 3, 1):
            dest = lax.rem(q + step, NQ)
            send(om.at[stream, dest], o2.at[stream, place], o2_send.at[stream, step], o2_recv.at[stream, place], at_q(dest))
        o2[stream, place] = om[stream, q]

    def out2_done(stream):
        for step in range(1, NQ):
            source = lax.rem(q + step, NQ)
            arrived(o2.at[stream, place_of(source)], o2_recv.at[stream, place_of(source)], at_q(source))

    def out1_send(stream):
        def spread_out(tile, carry):
            lanes = pl.ds(pl.multiple_of(tile * 128, 128), 128)
            for n in range(NQ):
                v32[n * 16 : (n + 1) * 16] = o2[stream, n, :, lanes].astype(jnp.float32)
            for n in range(NZ):
                back[stream, n, :, lanes] = v32[pl.ds(n, 16, stride=16), :].astype(jnp.bfloat16)

            @pl.when(tile < 4)
            def _():
                upper = pl.ds(pl.multiple_of(tile * 128 + LOW, 128), 128)
                for n in range(NZ):
                    back[stream, n, :, upper] = v32[pl.ds(n + 8, 16, stride=16), :].astype(jnp.bfloat16)

            return carry

        lax.fori_loop(0, 5, spread_out, 0)
        for n, step in enumerate((4, 3, 5, 2, 6, 1, 7)):
            target = lax.rem(z + step, NZ)
            send(
                back.at[stream, target], out_hbm.at[location_rows(z, stream)],
                o1_send.at[n, stream], o1_recv.at[z, stream], at_z(target),
            )
        copy = pltpu.make_async_copy(back.at[stream, z], out_hbm.at[location_rows(z, stream)], own_sem.at[2 + stream])
        copy.start()
        own.append(copy)

    def out1_done(stream):
        own[2 + stream].wait()
        for step in range(1, NZ):
            source = lax.rem(z + step, NZ)
            arrived(out_hbm.at[location_rows(source, stream)], o1_recv.at[source, stream], at_z(source))

    text_products()
    pl.semaphore_wait(barrier, NZ - 1 + NQ - 1 + 1)
    in1_send(0)
    text_send()
    send(wp_hbm.at[half_rows], wp_far.at[half_rows], w_send.at[0], w_recv.at[0], pair)
    in1_send(1)
    text_core_sum()
    text_x_sum()
    in1_done(0)
    in2_send(0)
    in1_done(1)
    in2_send(1)
    text_z_sum()
    for n in (2, 3, 4):
        loads[n].wait()
    in2_done(0)
    temporal_norm(0)
    loads[5].wait()
    text_y_sum()
    temporal(0)
    arrived(wp_far.at[half_rows], w_recv.at[0], pair)
    send(wp_far.at[half_rows], wp_far.at[half_rows], w_send.at[1], w_recv.at[1], sibling)
    text_z_gather()
    in2_done(1)
    temporal_norm(1)
    text_x_gather()
    temporal(1)
    loads[6].wait()
    loads[7].wait()
    arrived(wp_far.at[other_rows], w_recv.at[1], sibling)
    text_core_gather()
    mix(0)
    loads[8].wait()
    cross(0)
    mix(1)
    cross(1)
    out2_add(0)
    out2_send(0)
    out2_add(1)
    out2_send(1)
    out2_done(0)
    out1_send(0)
    out2_done(1)
    out1_send(1)
    out1_done(0)
    out1_done(1)
    drain()


def mega(length, x, shift, scale, gate, wqkv, wp, wcq, wcp, ckv, te):
    bf16, f32 = jnp.bfloat16, jnp.float32
    dma, vmem = pltpu.SemaphoreType.DMA, pltpu.VMEM
    return pl.pallas_call(
        kernel,
        out_shape=jax.ShapeDtypeStruct((TOKENS, D), bf16),
        in_specs=[pl.BlockSpec(memory_space=pltpu.SMEM)] + [pl.BlockSpec(memory_space=pltpu.HBM)] * 10,
        out_specs=pl.BlockSpec(memory_space=pltpu.HBM),
        scratch_shapes=[
            vmem((D,), f32), vmem((D,), f32), vmem((D,), f32),
            vmem((2, 32, WIDTH), bf16), vmem((32, TEXT_LEN), bf16),
            vmem((3, WIDTH, D), bf16), vmem((WIDTH, D), bf16), vmem((WIDTH, D), bf16),
            vmem((WIDTH, D), bf16), vmem((WIDTH, D), bf16),
            vmem((NZ, 2, 16, D), bf16), vmem((128, 128), f32), vmem((128, 128), f32), vmem((256, 128), f32),
            vmem((2, NQ, 16, LOW), bf16), vmem((2, NQ, 16, LOW), bf16),
            vmem((FRAMES, D), bf16), vmem((3, WIDTH, FRAMES), f32),
            vmem((2, 2, WIDTH, FRAMES), bf16), vmem((2, WIDTH, FRAMES), bf16),
            vmem((2, FRAMES, D), f32), vmem((FRAMES, D), f32),
            vmem((2, NQ, 16, LOW), bf16), vmem((2, NQ, 16, LOW), bf16),
            vmem((2, NQ, 16, LOW), bf16), vmem((2, NQ, 16, LOW), bf16), vmem((2, NZ, 16, D), bf16),
            vmem((32, 384), bf16), vmem((192, 16, 128), bf16), vmem((96, 16, 128), bf16), vmem((96, 16, 128), bf16),
            vmem((4, 24, 16, 128), bf16), vmem((24, 16, 128), bf16), vmem((8, 3, 16, 128), bf16),
            vmem((3, 16, 128), bf16), vmem((3, 16, 128), bf16), vmem((192, 16, 128), bf16),
            vmem((TEXT_ROWS, WIDTH), bf16), vmem((640, 384), f32),
            dma((9,)), dma((2,)), dma((2,)), dma((7, 2)), dma((8, 2)), dma((2, 16)), dma((2, 16)),
            dma((2, 2)), dma((2, 2)), dma((2, 16)), dma((2, 16)), dma((7, 2)), dma((8, 2)),
            dma((2,)), dma((2,)), dma((2, 4)), dma((2, 4)), dma((2, 8)), dma((2, 8)), dma((1,)), dma((1,)), dma((4,)),
        ],
        compiler_params=pltpu.CompilerParams(
            collective_id=0, has_side_effects=True, vmem_limit_bytes=60 * 1024 * 1024
        ),
        cost_estimate=pl.CostEstimate(flops=4_000_000_000, bytes_accessed=12_000_000, transcendentals=2_000_000),
        name="stdit",
    )(length, x, shift, scale, gate, wqkv, wp, wcq, wcp, ckv, te)


def body(
    video_latent, shift_temporal, scale_temporal, gate_temporal, temporal_qkv, temporal_proj,
    cross_query, cross_kv, cross_proj, text_embed, text_length,
):
    out = mega(
        text_length, video_latent.reshape(TOKENS, D),
        shift_temporal, scale_temporal, gate_temporal,
        jnp.transpose(temporal_qkv, (1, 2, 0)), temporal_proj, cross_query.T, cross_proj, cross_kv, text_embed.T,
    )
    return video_latent.astype(jnp.float32) + out.reshape(1, TOKENS, D).astype(jnp.float32)


def solution(mesh):
    return jax.shard_map(
        body,
        mesh=mesh,
        in_specs=(
            P("seq", None, None), P(), P(), P(), P(None, None, "tp"), P("tp", None), P(None, "tp"),
            P(None, "seq", "tp"), P("tp", None), P(None, "seq"), P(),
        ),
        out_specs=P("seq", None, None),
        check_vma=False,
    )
```

```python
import jax
import jax.numpy as jnp
from jax import lax
from jax.experimental import pallas as pl
from jax.experimental.pallas import tpu as pltpu
from jax.sharding import PartitionSpec as P

D = 1152
HD = 72
HEADS = 8
WIDTH = HEADS * HD
TOKENS = 256
FRAMES = 128
LOW, HIGH = 640, 512
NZ = 8
NQ = 16
TEXT_LEN = 300
TEXT_ROWS = 304
EXP_SCALE = HD ** (-0.5) * 1.4426950408889634
MESH = pl.DeviceIdType.MESH


def rows_of(index, size):
    return pl.ds(pl.multiple_of(index * size, size), size)


def dot(a, b, dims):
    return lax.dot_general(a, b, (dims, ((), ())), preferred_element_type=jnp.float32)


def attend(scores_of, value_of, visible, target):
    for group in range(0, HEADS, 4):
        scores = [scores_of(head) for head in range(group, group + 4)]
        weights, totals = [], []
        for score in scores:
            if visible is not None:
                score = jnp.where(visible, score, -1e30)
            top = jnp.max(score, axis=0, keepdims=True)
            weight = jnp.exp2((score - top) * EXP_SCALE)
            totals.append(1.0 / jnp.sum(weight, axis=0, keepdims=True))
            weights.append(weight.astype(jnp.bfloat16))
        mixed = [dot(value_of(group + n), weights[n], ((1,), (0,))) * totals[n] for n in range(4)]
        for n in (0, 2):
            target[(group + n) * HD : (group + n + 2) * HD] = jnp.concatenate(mixed[n : n + 2], axis=0).astype(jnp.bfloat16)


def kernel(
    length_ref, x_hbm, shift_hbm, scale_hbm, gate_hbm, wqkv_hbm, wp_hbm, wcq_hbm, wcp_hbm, ckv_hbm, te_hbm,
    out_hbm,
    shift_ref, scale_ref, gate_ref, ckv_ref, te_ref, wqkv, wp, wp_far, wcq, wcp, wcp_far,
    s1, t32, u32, v32, msg, xin, normed, qkv, asked, att, att_far, branch, partial, om, o2, back,
    te_pad, part, core_in, part_x, x_in, part_z, z_in, z_full, full, tk, tv,
    load_sem, w_send, w_recv, s1_send, s1_recv, s2_send, s2_recv,
    a_send, a_recv, o2_send, o2_recv, o1_send, o1_recv,
    c_send, c_recv, x_send, x_recv, z_send, z_recv, own_sem,
):
    seq, hi = lax.axis_index("seq"), lax.axis_index("tp")
    z, q = seq // NQ, lax.rem(seq, NQ)
    core, spot = lax.rem(q, 2), q // 2

    def other_y(index):
        return index + 2 - 4 * lax.rem(index // 2, 2)

    def group_of(index):
        return index + hi * (other_y(index) - index)

    def place_of(index):
        group = group_of(index)
        return lax.rem(group, 2) * 8 + group // 2

    def at_z(index):
        return (index * NQ + q, hi)

    def at_q(index):
        return (z * NQ + index, hi)

    def at_spot(index):
        return at_q(2 * index + core)

    pair = (z * NQ + other_y(q), 1 - hi)
    sibling = at_q(q + 1 - 2 * core)

    loads = [
        pltpu.make_async_copy(source, target, load_sem.at[n])
        for n, (source, target) in enumerate(
            (
                (te_hbm, te_ref), (ckv_hbm, ckv_ref), (shift_hbm, shift_ref), (scale_hbm, scale_ref),
                (gate_hbm, gate_ref), (wqkv_hbm, wqkv), (wp_hbm, wp), (wcq_hbm, wcq), (wcp_hbm, wcp),
            )
        )
    ]
    for load in loads:
        load.start()

    barrier = pltpu.get_barrier_semaphore()
    for step in range(1, NZ):
        pl.semaphore_signal(barrier, inc=1, device_id=at_z(lax.rem(z + step, NZ)), device_id_type=MESH)
    for step in range(1, NQ):
        pl.semaphore_signal(barrier, inc=1, device_id=at_q(lax.rem(q + step, NQ)), device_id_type=MESH)
    pl.semaphore_signal(barrier, inc=1, device_id=pair, device_id_type=MESH)

    def remote(source, target, send, recv, device):
        return pltpu.make_async_remote_copy(
            src_ref=source, dst_ref=target, send_sem=send, recv_sem=recv, device_id=device, device_id_type=MESH
        )

    sent = []

    def send(source, target, send_sem, recv_sem, device, when=None):
        copy = remote(source, target, send_sem, recv_sem, device)
        if when is None:
            copy.start()
        else:
            pl.when(when)(copy.start)
        sent.append((copy, when))

    def arrived(target, recv_sem, device, when=None):
        copy = remote(target, target, c_send.at[0], recv_sem, device)
        if when is None:
            copy.wait_recv()
        else:
            pl.when(when)(copy.wait_recv)

    def drain():
        for copy, when in sent:
            if when is None:
                copy.wait_send()
            else:
                pl.when(when)(copy.wait_send)
        sent.clear()

    def text_products():
        loads[0].wait()
        loads[1].wait()
        te_pad[...] = jnp.zeros_like(te_pad)
        te_pad[:, :TEXT_LEN] = te_ref[...]
        part[190:] = jnp.zeros((2, 16, 128), jnp.bfloat16)
        for which in range(2):
            product = lax.dot_general(
                te_pad[:, :TEXT_ROWS], ckv_ref[which], (((0,), (0,)), ((), ())), preferred_element_type=jnp.float32
            ).astype(jnp.bfloat16)
            product = jnp.concatenate([product, jnp.zeros((TEXT_ROWS, 64), jnp.bfloat16)], axis=1)
            for r in range(TEXT_ROWS // 16):
                for tile in range(5):
                    part[r * 10 + which * 5 + tile] = product[r * 16 : r * 16 + 16, tile * 128 : tile * 128 + 128]

    def text_send():
        send(part.at[pl.ds(96 - 96 * core, 96)], core_in, c_send.at[0], c_recv.at[0], sibling)

    def text_core_sum():
        arrived(core_in, c_recv.at[0], sibling)
        part_x[...] = (part[pl.ds(96 * core, 96)].astype(jnp.float32) + core_in[...].astype(jnp.float32)).astype(jnp.bfloat16)
        for step in (4, 6, 2, 5, 3, 7, 1):
            target = lax.rem(spot + step, 8)
            send(part_x.at[pl.ds(12 * target, 12)], x_in.at[spot], x_send.at[0, step], x_recv.at[0, spot], at_spot(target))

    def text_x_sum():
        total = part_x[pl.ds(12 * spot, 12)].astype(jnp.float32)
        for step in range(1, 8):
            source = lax.rem(spot + step, 8)
            arrived(x_in.at[source], x_recv.at[0, source], at_spot(source))
            total += x_in[source].astype(jnp.float32)
        part_z[...] = total.reshape(24, 8, 128)
        for step in (4, 3, 5, 2, 6, 1, 7):
            target = lax.rem(z + step, NZ)
            send(part_z.at[pl.ds(3 * target, 3)], z_in.at[z], z_send.at[0, step], z_recv.at[0, z], at_z(target))

    def text_z_sum():
        total = part_z[pl.ds(3 * z, 3)]
        for step in range(1, NZ):
            source = lax.rem(z + step, NZ)
            arrived(z_in.at[source], z_recv.at[0, source], at_z(source))
            total += z_in[source]
        mine = z_full.at[pl.ds(3 * z, 3)]
        mine[...] = total
        for step in (4, 3, 5, 2, 6, 1, 7):
            send(mine, mine, z_send.at[1, step], z_recv.at[1, z], at_z(lax.rem(z + step, NZ)))

    def text_z_gather():
        for step in range(1, NZ):
            source = lax.rem(z + step, NZ)
            arrived(z_full.at[pl.ds(3 * source, 3)], z_recv.at[1, source], at_z(source))
        mine = full.at[pl.ds(96 * core + 12 * spot, 12)]
        mine[...] = z_full[...].reshape(12, 16, 128).astype(jnp.bfloat16)
        for step in (4, 6, 2, 5, 3, 7, 1):
            send(mine, mine, x_send.at[1, step], x_recv.at[1, spot], at_spot(lax.rem(spot + step, 8)))

    def text_x_gather():
        for step in range(1, 8):
            source = lax.rem(spot + step, 8)
            arrived(full.at[pl.ds(96 * core + 12 * source, 12)], x_recv.at[1, source], at_spot(source))
        mine = full.at[pl.ds(96 * core, 96)]
        send(mine, mine, c_send.at[1], c_recv.at[1], sibling)

    def text_core_gather():
        arrived(full.at[pl.ds(96 - 96 * core, 96)], c_recv.at[1], sibling)
        for tile in range(5):
            width = min(128, WIDTH - tile * 128)
            rows = []
            for r in range(TEXT_ROWS // 16):
                tk[r * 16 : r * 16 + 16, tile * 128 : tile * 128 + width] = full[r * 10 + tile][:, :width]
                rows.append(full[r * 10 + 5 + tile].astype(jnp.float32))
            rows.append(jnp.zeros((384 - TEXT_ROWS, 128), jnp.float32))
            tv[tile * 128 : (tile + 1) * 128] = jnp.concatenate(rows, axis=0).T

    half_rows = pl.ds(pl.multiple_of(core * 288, 288), 288)
    odd_x = lax.rem(q // 4, 2)
    beside = at_q(q + 4 - 8 * odd_x)
    quarter_rows = pl.ds(pl.multiple_of(core * 288 + odd_x * 144, 16), 144)
    beside_rows = pl.ds(pl.multiple_of(core * 288 + 144 - odd_x * 144, 16), 144)
    other_rows = pl.ds(pl.multiple_of(288 - core * 288, 288), 288)
    own = []

    def location_rows(index, stream):
        return pl.ds(pl.multiple_of(index * 32 + stream * 16, 16), 16)

    def in1_send(stream):
        for n, step in enumerate((4, 3, 5, 2, 6, 1, 7)):
            target = lax.rem(z + step, NZ)
            send(
                x_hbm.at[location_rows(target, stream)],
                s1.at[z, stream], s1_send.at[n, stream], s1_recv.at[z, stream], at_z(target),
            )
        copy = pltpu.make_async_copy(x_hbm.at[location_rows(z, stream)], s1.at[z, stream], own_sem.at[stream])
        copy.start()
        own.append(copy)

    def in1_done(stream):
        own[stream].wait()
        for step in range(1, NZ):
            source = lax.rem(z + step, NZ)
            arrived(s1.at[source, stream], s1_recv.at[source, stream], at_z(source))

    def in2_send(stream):
        def spread_in(tile, carry):
            lanes = pl.ds(pl.multiple_of(tile * 128, 128), 128)
            upper = pl.ds(pl.multiple_of(lax.rem(tile + 5, 9) * 128, 128), 128)
            for n in range(NZ):
                t32[n * 16 : (n + 1) * 16] = s1[n, stream, :, lanes].astype(jnp.float32)
                u32[n * 16 : (n + 1) * 16] = s1[n, stream, :, upper].astype(jnp.float32)
            for n in range(NQ):
                both = jnp.concatenate([t32[pl.ds(n, 8, stride=16), :], u32[pl.ds(n, 8, stride=16), :]], axis=0)
                msg[stream, n, :, lanes] = both.astype(jnp.bfloat16)
            return carry

        lax.fori_loop(0, 5, spread_in, 0)
        for step in (8, 4, 12, 10, 6, 14, 2, 9, 5, 13, 11, 7, 15, 3, 1):
            dest = lax.rem(q + step, NQ)
            send(msg.at[stream, place_of(dest)], xin.at[stream, q], s2_send.at[stream, step], s2_recv.at[stream, q], at_q(dest))
        xin[stream, q] = msg[stream, place_of(q)]

    def in2_done(stream):
        for step in range(1, NQ):
            source = lax.rem(q + step, NQ)
            arrived(xin.at[stream, source], s2_recv.at[stream, source], at_q(source))

    def latent_rows(stream, n):
        first, second = xin[stream, 2 * n].astype(jnp.float32), xin[stream, 2 * n + 1].astype(jnp.float32)
        low = jnp.concatenate([first[:8], second[:8]], axis=0)
        high = jnp.concatenate([first[8:, :HIGH], second[8:, :HIGH]], axis=0)
        return jnp.concatenate([low, high], axis=1)

    def temporal_norm(stream):
        def norm_rows(n, carry):
            values = latent_rows(stream, n)
            center = jnp.mean(values, axis=-1, keepdims=True)
            values = values - center
            spread = jnp.mean(jnp.square(values), axis=-1, keepdims=True)
            values = values * lax.rsqrt(spread + 1e-06) * (1.0 + scale_ref[...].reshape(1, D)) + shift_ref[...].reshape(1, D)
            normed[rows_of(n, 16)] = values.astype(jnp.bfloat16)
            return carry

        lax.fori_loop(0, 8, norm_rows, 0, unroll=2)

    def head_rows(which, head):
        return qkv[which, head * HD : (head + 1) * HD].astype(jnp.bfloat16)

    def temporal(stream):
        def project(n, carry):
            qkv[n] = dot(wqkv[n], normed[...], ((1,), (1,)))
            return carry

        lax.fori_loop(0, 3, project, 0)
        attend(
            lambda head: dot(head_rows(1, head), head_rows(0, head), ((0,), (0,))),
            lambda head: head_rows(2, head), None, att.at[0, stream],
        )
        send(att.at[0, stream], att_far.at[0, stream], a_send.at[0, stream], a_recv.at[0, stream], pair)

    def mix(stream):
        branch[stream] = dot(att[0, stream], wp[...], ((0,), (0,)))
        arrived(att_far.at[0, stream], a_recv.at[0, stream], pair)
        total = branch[stream] + dot(att_far[0, stream], wp_far[...], ((0,), (0,)))
        branch[stream] = total * gate_ref[...].reshape(1, D)

        def mix_rows(n, carry):
            rows = rows_of(n, 16)
            normed[rows] = (latent_rows(stream, n) + branch[stream, rows]).astype(jnp.bfloat16)
            return carry

        lax.fori_loop(0, 8, mix_rows, 0, unroll=2)
        asked[stream] = dot(wcq[...], normed[...], ((1,), (1,)))

    def cross(stream):
        row = lax.broadcasted_iota(jnp.int32, (TEXT_ROWS, FRAMES), 0)

        def scores_of(head):
            low, high = head * HD, (head + 1) * HD
            start, end = low // 128 * 128, min(-(-high // 128) * 128, WIDTH)
            place = lax.broadcasted_iota(jnp.int32, (end - start, FRAMES), 0) + start
            query = jnp.where((place >= low) & (place < high), asked[stream, start:end], 0.0).astype(jnp.bfloat16)
            return dot(tk[:, start:end], query, ((1,), (0,)))

        def value_of(head):
            return tv[head * HD : (head + 1) * HD, :TEXT_ROWS].astype(jnp.bfloat16)

        attend(scores_of, value_of, row < length_ref[0], att.at[1, stream])
        send(att.at[1, stream], att_far.at[1, stream], a_send.at[1, stream], a_recv.at[1, stream], pair)
        partial[stream] = dot(att[1, stream], wcp[...], ((0,), (0,)))

    def fold(rows):
        high = jnp.concatenate([rows[:, LOW:], jnp.zeros((8, LOW - HIGH), jnp.float32)], axis=1)
        return jnp.concatenate([rows[:, :LOW], high], axis=0)

    def out2_add(stream):
        arrived(att_far.at[1, stream], a_recv.at[1, stream], pair)
        partial[stream] += dot(att_far[1, stream], wcp_far[...], ((0,), (0,)))

        def add_rows(n, carry):
            om[stream, n] = fold(branch[stream, rows_of(n, 8)] + partial[stream, rows_of(n, 8)]).astype(jnp.bfloat16)
            return carry

        lax.fori_loop(0, NQ, add_rows, 0, unroll=2)

    def out2_send(stream):
        place = place_of(q)
        for step in (8, 4, 12, 10, 6, 14, 2, 9, 5, 13, 11, 7, 15, 3, 1):
            dest = lax.rem(q + step, NQ)
            send(om.at[stream, dest], o2.at[stream, place], o2_send.at[stream, step], o2_recv.at[stream, place], at_q(dest))
        o2[stream, place] = om[stream, q]

    def out2_done(stream):
        for step in range(1, NQ):
            source = lax.rem(q + step, NQ)
            arrived(o2.at[stream, place_of(source)], o2_recv.at[stream, place_of(source)], at_q(source))

    def out1_send(stream):
        def spread_out(tile, carry):
            lanes = pl.ds(pl.multiple_of(tile * 128, 128), 128)
            for n in range(NQ):
                v32[n * 16 : (n + 1) * 16] = o2[stream, n, :, lanes].astype(jnp.float32)
            for n in range(NZ):
                back[stream, n, :, lanes] = v32[pl.ds(n, 16, stride=16), :].astype(jnp.bfloat16)

            @pl.when(tile < 4)
            def _():
                upper = pl.ds(pl.multiple_of(tile * 128 + LOW, 128), 128)
                for n in range(NZ):
                    back[stream, n, :, upper] = v32[pl.ds(n + 8, 16, stride=16), :].astype(jnp.bfloat16)

            return carry

        lax.fori_loop(0, 5, spread_out, 0)
        for n, step in enumerate((4, 3, 5, 2, 6, 1, 7)):
            target = lax.rem(z + step, NZ)
            send(
                back.at[stream, target], out_hbm.at[location_rows(z, stream)],
                o1_send.at[n, stream], o1_recv.at[z, stream], at_z(target),
            )
        copy = pltpu.make_async_copy(back.at[stream, z], out_hbm.at[location_rows(z, stream)], own_sem.at[2 + stream])
        copy.start()
        own.append(copy)

    def out1_done(stream):
        own[2 + stream].wait()
        for step in range(1, NZ):
            source = lax.rem(z + step, NZ)
            arrived(out_hbm.at[location_rows(source, stream)], o1_recv.at[source, stream], at_z(source))

    text_products()
    pl.semaphore_wait(barrier, NZ - 1 + NQ - 1 + 1)
    text_send()
    in1_send(0)
    send(wp_hbm.at[half_rows], wp_far.at[half_rows], w_send.at[0], w_recv.at[0], pair)
    in1_send(1)
    send(wcp_hbm.at[quarter_rows], wcp_far.at[quarter_rows], w_send.at[2], w_recv.at[2], pair)
    text_core_sum()
    in1_done(0)
    in2_send(0)
    text_x_sum()
    in1_done(1)
    in2_send(1)
    text_z_sum()
    for n in (2, 3, 4):
        loads[n].wait()
    in2_done(0)
    temporal_norm(0)
    loads[5].wait()
    temporal(0)
    text_z_gather()
    arrived(wp_far.at[half_rows], w_recv.at[0], pair)
    send(wp_far.at[half_rows], wp_far.at[half_rows], w_send.at[1], w_recv.at[1], sibling)
    in2_done(1)
    temporal_norm(1)
    temporal(1)
    arrived(wcp_far.at[quarter_rows], w_recv.at[2], pair)
    send(wcp_far.at[quarter_rows], wcp_far.at[quarter_rows], w_send.at[4], w_recv.at[4], beside)
    text_x_gather()
    loads[6].wait()
    loads[7].wait()
    arrived(wp_far.at[other_rows], w_recv.at[1], sibling)
    mix(0)
    loads[8].wait()
    text_core_gather()
    cross(0)
    arrived(wcp_far.at[beside_rows], w_recv.at[4], beside)
    send(wcp_far.at[half_rows], wcp_far.at[half_rows], w_send.at[3], w_recv.at[3], sibling)
    mix(1)
    arrived(wcp_far.at[other_rows], w_recv.at[3], sibling)
    out2_add(0)
    out2_send(0)
    cross(1)
    out2_add(1)
    out2_send(1)
    out2_done(0)
    out1_send(0)
    out2_done(1)
    out1_send(1)
    out1_done(0)
    out1_done(1)
    drain()


def mega(length, x, shift, scale, gate, wqkv, wp, wcq, wcp, ckv, te):
    bf16, f32 = jnp.bfloat16, jnp.float32
    dma, vmem = pltpu.SemaphoreType.DMA, pltpu.VMEM
    return pl.pallas_call(
        kernel,
        out_shape=jax.ShapeDtypeStruct((TOKENS, D), bf16),
        in_specs=[pl.BlockSpec(memory_space=pltpu.SMEM)] + [pl.BlockSpec(memory_space=pltpu.HBM)] * 10,
        out_specs=pl.BlockSpec(memory_space=pltpu.HBM),
        scratch_shapes=[
            vmem((D,), f32), vmem((D,), f32), vmem((D,), f32),
            vmem((2, 32, WIDTH), bf16), vmem((32, TEXT_LEN), bf16),
            vmem((3, WIDTH, D), bf16), vmem((WIDTH, D), bf16), vmem((WIDTH, D), bf16),
            vmem((WIDTH, D), bf16), vmem((WIDTH, D), bf16), vmem((WIDTH, D), bf16),
            vmem((NZ, 2, 16, D), bf16), vmem((128, 128), f32), vmem((128, 128), f32), vmem((256, 128), f32),
            vmem((2, NQ, 16, LOW), bf16), vmem((2, NQ, 16, LOW), bf16),
            vmem((FRAMES, D), bf16), vmem((3, WIDTH, FRAMES), f32), vmem((2, WIDTH, FRAMES), f32),
            vmem((2, 2, WIDTH, FRAMES), bf16), vmem((2, 2, WIDTH, FRAMES), bf16),
            vmem((2, FRAMES, D), f32), vmem((2, FRAMES, D), f32),
            vmem((2, NQ, 16, LOW), bf16), vmem((2, NQ, 16, LOW), bf16), vmem((2, NZ, 16, D), bf16),
            vmem((32, 384), bf16), vmem((192, 16, 128), bf16), vmem((96, 16, 128), bf16), vmem((96, 16, 128), bf16),
            vmem((8, 12, 16, 128), bf16), vmem((24, 8, 128), f32), vmem((8, 3, 8, 128), f32), vmem((24, 8, 128), f32),
            vmem((192, 16, 128), bf16),
            vmem((TEXT_ROWS, WIDTH), bf16), vmem((640, 384), f32),
            dma((9,)), dma((6,)), dma((6,)), dma((7, 2)), dma((8, 2)), dma((2, 16)), dma((2, 16)),
            dma((2, 2)), dma((2, 2)), dma((2, 16)), dma((2, 16)), dma((7, 2)), dma((8, 2)),
            dma((2,)), dma((2,)), dma((2, 8)), dma((2, 8)), dma((2, 8)), dma((2, 8)), dma((4,)),
        ],
        compiler_params=pltpu.CompilerParams(
            collective_id=0, has_side_effects=True, vmem_limit_bytes=60 * 1024 * 1024
        ),
        cost_estimate=pl.CostEstimate(flops=4_000_000_000, bytes_accessed=12_000_000, transcendentals=2_000_000),
        name="stdit",
    )(length, x, shift, scale, gate, wqkv, wp, wcq, wcp, ckv, te)


def body(
    video_latent, shift_temporal, scale_temporal, gate_temporal, temporal_qkv, temporal_proj,
    cross_query, cross_kv, cross_proj, text_embed, text_length,
):
    out = mega(
        text_length, video_latent.reshape(TOKENS, D),
        shift_temporal, scale_temporal, gate_temporal,
        jnp.transpose(temporal_qkv, (1, 2, 0)), temporal_proj, cross_query.T, cross_proj, cross_kv, text_embed.T,
    )
    return video_latent.astype(jnp.float32) + out.reshape(1, TOKENS, D).astype(jnp.float32)


def solution(mesh):
    return jax.shard_map(
        body,
        mesh=mesh,
        in_specs=(
            P("seq", None, None), P(), P(), P(), P(None, None, "tp"), P("tp", None), P(None, "tp"),
            P(None, "seq", "tp"), P("tp", None), P(None, "seq"), P(),
        ),
        out_specs=P("seq", None, None),
        check_vma=False,
    )
```

```python
import jax
import jax.numpy as jnp
from jax import lax
from jax.experimental import pallas as pl
from jax.experimental.pallas import tpu as pltpu
from jax.sharding import PartitionSpec as P

D = 1152
HD = 72
HEADS = 8
WIDTH = HEADS * HD
TOKENS = 256
FRAMES = 128
LOW, HIGH = 640, 512
NZ = 8
NQ = 16
TEXT_LEN = 300
TEXT_ROWS = 304
EXP_SCALE = HD ** (-0.5) * 1.4426950408889634
MESH = pl.DeviceIdType.MESH


def rows_of(index, size):
    return pl.ds(pl.multiple_of(index * size, size), size)


def dot(a, b, dims):
    return lax.dot_general(a, b, (dims, ((), ())), preferred_element_type=jnp.float32)


def attend(scores_of, value_of, visible, target, after):
    for group in range(0, HEADS, 4):
        scores = [scores_of(head) for head in range(group, group + 4)]
        weights, totals = [], []
        for score in scores:
            if visible is not None:
                score = jnp.where(visible, score, -1e30)
            top = jnp.max(score, axis=0, keepdims=True)
            weight = jnp.exp2((score - top) * EXP_SCALE)
            totals.append(1.0 / jnp.sum(weight, axis=0, keepdims=True))
            weights.append(weight.astype(jnp.bfloat16))
        mixed = [dot(value_of(group + n), weights[n], ((1,), (0,))) * totals[n] for n in range(4)]
        for n in (0, 2):
            target[(group + n) * HD : (group + n + 2) * HD] = jnp.concatenate(mixed[n : n + 2], axis=0).astype(jnp.bfloat16)
        after(group // 4)


def kernel(
    length_ref, x_hbm, shift_hbm, scale_hbm, gate_hbm, wqkv_hbm, wp_hbm, wcq_hbm, wcp_hbm, ckv_hbm, te_hbm,
    out_hbm,
    shift_ref, scale_ref, gate_ref, ckv_ref, te_ref, wqkv, wp, wp_far, wcq, wcp, wcp_far,
    s1, t32, u32, v32, msg, xin, normed, qkv, asked, att, att_far, branch, partial, om, o2, back,
    te_pad, part, core_in, part_x, x_in, part_z, z_in, z_full, full, tk, tv,
    load_sem, w_send, w_recv, s1_send, s1_recv, s2_send, s2_recv,
    a_send, a_recv, o2_send, o2_recv, o1_send, o1_recv,
    c_send, c_recv, x_send, x_recv, z_send, z_recv, own_sem,
):
    seq, hi = lax.axis_index("seq"), lax.axis_index("tp")
    z, q = seq // NQ, lax.rem(seq, NQ)
    core, spot = lax.rem(q, 2), q // 2

    def other_y(index):
        return index + 2 - 4 * lax.rem(index // 2, 2)

    def group_of(index):
        return index + hi * (other_y(index) - index)

    def place_of(index):
        group = group_of(index)
        return lax.rem(group, 2) * 8 + group // 2

    def at_z(index):
        return (index * NQ + q, hi)

    def at_q(index):
        return (z * NQ + index, hi)

    def at_spot(index):
        return at_q(2 * index + core)

    pair = (z * NQ + other_y(q), 1 - hi)
    sibling = at_q(q + 1 - 2 * core)

    loads = [
        pltpu.make_async_copy(source, target, load_sem.at[n])
        for n, (source, target) in enumerate(
            (
                (te_hbm, te_ref), (ckv_hbm, ckv_ref), (shift_hbm, shift_ref), (scale_hbm, scale_ref),
                (gate_hbm, gate_ref), (wqkv_hbm, wqkv), (wp_hbm, wp), (wcq_hbm, wcq), (wcp_hbm, wcp),
            )
        )
    ]
    for load in loads:
        load.start()

    barrier = pltpu.get_barrier_semaphore()
    for step in range(1, NZ):
        pl.semaphore_signal(barrier, inc=1, device_id=at_z(lax.rem(z + step, NZ)), device_id_type=MESH)
    for step in range(1, NQ):
        pl.semaphore_signal(barrier, inc=1, device_id=at_q(lax.rem(q + step, NQ)), device_id_type=MESH)
    pl.semaphore_signal(barrier, inc=1, device_id=pair, device_id_type=MESH)

    def remote(source, target, send, recv, device):
        return pltpu.make_async_remote_copy(
            src_ref=source, dst_ref=target, send_sem=send, recv_sem=recv, device_id=device, device_id_type=MESH
        )

    sent = []

    def send(source, target, send_sem, recv_sem, device, when=None):
        copy = remote(source, target, send_sem, recv_sem, device)
        if when is None:
            copy.start()
        else:
            pl.when(when)(copy.start)
        sent.append((copy, when))

    def arrived(target, recv_sem, device, when=None):
        copy = remote(target, target, c_send.at[0], recv_sem, device)
        if when is None:
            copy.wait_recv()
        else:
            pl.when(when)(copy.wait_recv)

    def drain():
        for copy, when in sent:
            if when is None:
                copy.wait_send()
            else:
                pl.when(when)(copy.wait_send)
        sent.clear()

    def text_products():
        loads[0].wait()
        loads[1].wait()
        te_pad[...] = jnp.zeros_like(te_pad)
        te_pad[:, :TEXT_LEN] = te_ref[...]
        part[190:] = jnp.zeros((2, 16, 128), jnp.bfloat16)
        for which in range(2):
            product = lax.dot_general(
                te_pad[:, :TEXT_ROWS], ckv_ref[which], (((0,), (0,)), ((), ())), preferred_element_type=jnp.float32
            ).astype(jnp.bfloat16)
            product = jnp.concatenate([product, jnp.zeros((TEXT_ROWS, 64), jnp.bfloat16)], axis=1)
            for r in range(TEXT_ROWS // 16):
                for tile in range(5):
                    part[r * 10 + which * 5 + tile] = product[r * 16 : r * 16 + 16, tile * 128 : tile * 128 + 128]

    def text_send():
        send(part.at[pl.ds(96 - 96 * core, 96)], core_in, c_send.at[0], c_recv.at[0], sibling)

    def text_core_sum():
        arrived(core_in, c_recv.at[0], sibling)
        part_x[...] = (part[pl.ds(96 * core, 96)].astype(jnp.float32) + core_in[...].astype(jnp.float32)).astype(jnp.bfloat16)
        for step in (4, 6, 2, 5, 3, 7, 1):
            target = lax.rem(spot + step, 8)
            send(part_x.at[pl.ds(12 * target, 12)], x_in.at[spot], x_send.at[0, step], x_recv.at[0, spot], at_spot(target))

    def text_x_sum():
        total = part_x[pl.ds(12 * spot, 12)].astype(jnp.float32)
        for step in range(1, 8):
            source = lax.rem(spot + step, 8)
            arrived(x_in.at[source], x_recv.at[0, source], at_spot(source))
            total += x_in[source].astype(jnp.float32)
        part_z[...] = total.reshape(24, 8, 128)
        for step in (4, 3, 5, 2, 6, 1, 7):
            target = lax.rem(z + step, NZ)
            send(part_z.at[pl.ds(3 * target, 3)], z_in.at[z], z_send.at[0, step], z_recv.at[0, z], at_z(target))

    def text_z_sum():
        total = part_z[pl.ds(3 * z, 3)]
        for step in range(1, NZ):
            source = lax.rem(z + step, NZ)
            arrived(z_in.at[source], z_recv.at[0, source], at_z(source))
            total += z_in[source]
        mine = z_full.at[pl.ds(3 * z, 3)]
        mine[...] = total
        for step in (4, 3, 5, 2, 6, 1, 7):
            send(mine, mine, z_send.at[1, step], z_recv.at[1, z], at_z(lax.rem(z + step, NZ)))

    def text_z_gather():
        for step in range(1, NZ):
            source = lax.rem(z + step, NZ)
            arrived(z_full.at[pl.ds(3 * source, 3)], z_recv.at[1, source], at_z(source))
        mine = full.at[pl.ds(96 * core + 12 * spot, 12)]
        mine[...] = z_full[...].reshape(12, 16, 128).astype(jnp.bfloat16)
        for step in (4, 6, 2, 5, 3, 7, 1):
            send(mine, mine, x_send.at[1, step], x_recv.at[1, spot], at_spot(lax.rem(spot + step, 8)))

    def text_x_gather():
        for step in range(1, 8):
            source = lax.rem(spot + step, 8)
            arrived(full.at[pl.ds(96 * core + 12 * source, 12)], x_recv.at[1, source], at_spot(source))
        mine = full.at[pl.ds(96 * core, 96)]
        send(mine, mine, c_send.at[1], c_recv.at[1], sibling)

    def text_core_gather():
        arrived(full.at[pl.ds(96 - 96 * core, 96)], c_recv.at[1], sibling)
        for tile in range(5):
            width = min(128, WIDTH - tile * 128)
            rows = []
            for r in range(TEXT_ROWS // 16):
                tk[r * 16 : r * 16 + 16, tile * 128 : tile * 128 + width] = full[r * 10 + tile][:, :width]
                rows.append(full[r * 10 + 5 + tile].astype(jnp.float32))
            rows.append(jnp.zeros((384 - TEXT_ROWS, 128), jnp.float32))
            tv[tile * 128 : (tile + 1) * 128] = jnp.concatenate(rows, axis=0).T

    half_rows = pl.ds(pl.multiple_of(core * 288, 288), 288)
    odd_x = lax.rem(q // 4, 2)
    beside = at_q(q + 4 - 8 * odd_x)
    quarter_rows = pl.ds(pl.multiple_of(core * 288 + odd_x * 144, 16), 144)
    beside_rows = pl.ds(pl.multiple_of(core * 288 + 144 - odd_x * 144, 16), 144)
    other_quarters = [
        pl.ds(pl.multiple_of(288 - core * 288 + start, 16), 144) for start in (odd_x * 144, 144 - odd_x * 144)
    ]
    other_rows = pl.ds(pl.multiple_of(288 - core * 288, 288), 288)
    own = []

    def location_rows(index, stream):
        return pl.ds(pl.multiple_of(index * 32 + stream * 16, 16), 16)

    def in1_send(stream):
        for n, step in enumerate((4, 3, 5, 2, 6, 1, 7)):
            target = lax.rem(z + step, NZ)
            send(
                x_hbm.at[location_rows(target, stream)],
                s1.at[z, stream], s1_send.at[n, stream], s1_recv.at[z, stream], at_z(target),
            )
        copy = pltpu.make_async_copy(x_hbm.at[location_rows(z, stream)], s1.at[z, stream], own_sem.at[stream])
        copy.start()
        own.append(copy)

    def in1_done(stream):
        own[stream].wait()
        for step in range(1, NZ):
            source = lax.rem(z + step, NZ)
            arrived(s1.at[source, stream], s1_recv.at[source, stream], at_z(source))

    def in2_send(stream):
        def spread_in(tile, carry):
            lanes = pl.ds(pl.multiple_of(tile * 128, 128), 128)
            upper = pl.ds(pl.multiple_of(lax.rem(tile + 5, 9) * 128, 128), 128)
            for n in range(NZ):
                t32[n * 16 : (n + 1) * 16] = s1[n, stream, :, lanes].astype(jnp.float32)
                u32[n * 16 : (n + 1) * 16] = s1[n, stream, :, upper].astype(jnp.float32)
            for n in range(NQ):
                both = jnp.concatenate([t32[pl.ds(n, 8, stride=16), :], u32[pl.ds(n, 8, stride=16), :]], axis=0)
                msg[stream, n, :, lanes] = both.astype(jnp.bfloat16)
            return carry

        lax.fori_loop(0, 5, spread_in, 0)
        for step in (8, 4, 12, 10, 6, 14, 2, 9, 5, 13, 11, 7, 15, 3, 1):
            dest = lax.rem(q + step, NQ)
            send(msg.at[stream, place_of(dest)], xin.at[stream, q], s2_send.at[stream, step], s2_recv.at[stream, q], at_q(dest))
        xin[stream, q] = msg[stream, place_of(q)]

    def in2_done(stream):
        for step in range(1, NQ):
            source = lax.rem(q + step, NQ)
            arrived(xin.at[stream, source], s2_recv.at[stream, source], at_q(source))

    def latent_rows(stream, n):
        first, second = xin[stream, 2 * n].astype(jnp.float32), xin[stream, 2 * n + 1].astype(jnp.float32)
        low = jnp.concatenate([first[:8], second[:8]], axis=0)
        high = jnp.concatenate([first[8:, :HIGH], second[8:, :HIGH]], axis=0)
        return jnp.concatenate([low, high], axis=1)

    def temporal_norm(stream):
        def norm_rows(n, carry):
            values = latent_rows(stream, n)
            center = jnp.mean(values, axis=-1, keepdims=True)
            values = values - center
            spread = jnp.mean(jnp.square(values), axis=-1, keepdims=True)
            values = values * lax.rsqrt(spread + 1e-06) * (1.0 + scale_ref[...].reshape(1, D)) + shift_ref[...].reshape(1, D)
            normed[rows_of(n, 16)] = values.astype(jnp.bfloat16)
            return carry

        lax.fori_loop(0, 8, norm_rows, 0, unroll=2)

    def head_rows(which, head):
        return qkv[which, head * HD : (head + 1) * HD].astype(jnp.bfloat16)

    def temporal(stream):
        def project(n, carry):
            qkv[n] = dot(wqkv[n], normed[...], ((1,), (1,)))
            return carry

        lax.fori_loop(0, 3, project, 0)
        attend(
            lambda head: dot(head_rows(1, head), head_rows(0, head), ((0,), (0,))),
            lambda head: head_rows(2, head), None, att.at[0, stream], lambda half: swap(0, stream, half),
        )

    def swap(kind, stream, half):
        rows = pl.ds(half * 288, 288)
        send(
            att.at[kind, stream, rows], att_far.at[kind, stream, rows],
            a_send.at[kind, stream, half], a_recv.at[kind, stream, half], pair,
        )

    def swapped(kind, stream):
        for half in range(2):
            arrived(att_far.at[kind, stream, pl.ds(half * 288, 288)], a_recv.at[kind, stream, half], pair)

    def mix(stream):
        branch[stream] = dot(att[0, stream], wp[...], ((0,), (0,)))
        swapped(0, stream)
        total = branch[stream] + dot(att_far[0, stream], wp_far[...], ((0,), (0,)))
        branch[stream] = total * gate_ref[...].reshape(1, D)

        def mix_rows(n, carry):
            rows = rows_of(n, 16)
            normed[rows] = (latent_rows(stream, n) + branch[stream, rows]).astype(jnp.bfloat16)
            return carry

        lax.fori_loop(0, 8, mix_rows, 0, unroll=2)
        asked[stream] = dot(wcq[...], normed[...], ((1,), (1,)))

    def cross(stream):
        row = lax.broadcasted_iota(jnp.int32, (TEXT_ROWS, FRAMES), 0)

        def scores_of(head):
            low, high = head * HD, (head + 1) * HD
            start, end = low // 128 * 128, min(-(-high // 128) * 128, WIDTH)
            place = lax.broadcasted_iota(jnp.int32, (end - start, FRAMES), 0) + start
            query = jnp.where((place >= low) & (place < high), asked[stream, start:end], 0.0).astype(jnp.bfloat16)
            return dot(tk[:, start:end], query, ((1,), (0,)))

        def value_of(head):
            return tv[head * HD : (head + 1) * HD, :TEXT_ROWS].astype(jnp.bfloat16)

        attend(scores_of, value_of, row < length_ref[0], att.at[1, stream], lambda half: swap(1, stream, half))
        partial[stream] = dot(att[1, stream], wcp[...], ((0,), (0,)))

    def fold(rows):
        high = jnp.concatenate([rows[:, LOW:], jnp.zeros((8, LOW - HIGH), jnp.float32)], axis=1)
        return jnp.concatenate([rows[:, :LOW], high], axis=0)

    def out2_add(stream):
        swapped(1, stream)
        partial[stream] += dot(att_far[1, stream], wcp_far[...], ((0,), (0,)))

        def add_rows(n, carry):
            om[stream, n] = fold(branch[stream, rows_of(n, 8)] + partial[stream, rows_of(n, 8)]).astype(jnp.bfloat16)
            return carry

        lax.fori_loop(0, NQ, add_rows, 0, unroll=2)

    def out2_send(stream):
        place = place_of(q)
        for first in range(2):
            for step in (4, 6, 2, 5, 3, 7, 1, 0):
                dest = 2 * lax.rem(spot + step, 8) + first
                when = None if step else core != first
                send(
                    om.at[stream, dest], o2.at[stream, place],
                    o2_send.at[stream, first * 8 + step], o2_recv.at[stream, place], at_q(dest), when,
                )
        o2[stream, place] = om[stream, q]

    def out2_done(stream):
        for step in range(1, NQ):
            source = lax.rem(q + step, NQ)
            arrived(o2.at[stream, place_of(source)], o2_recv.at[stream, place_of(source)], at_q(source))

    def out1_send(stream):
        def spread_out(tile, carry):
            lanes = pl.ds(pl.multiple_of(tile * 128, 128), 128)
            for n in range(NQ):
                v32[n * 16 : (n + 1) * 16] = o2[stream, n, :, lanes].astype(jnp.float32)
            for n in range(NZ):
                back[stream, n, :, lanes] = v32[pl.ds(n, 16, stride=16), :].astype(jnp.bfloat16)

            @pl.when(tile < 4)
            def _():
                upper = pl.ds(pl.multiple_of(tile * 128 + LOW, 128), 128)
                for n in range(NZ):
                    back[stream, n, :, upper] = v32[pl.ds(n + 8, 16, stride=16), :].astype(jnp.bfloat16)

            return carry

        lax.fori_loop(0, 5, spread_out, 0)
        for n, step in enumerate((4, 3, 5, 2, 6, 1, 7)):
            target = lax.rem(z + step, NZ)
            send(
                back.at[stream, target], out_hbm.at[location_rows(z, stream)],
                o1_send.at[n, stream], o1_recv.at[z, stream], at_z(target),
            )
        copy = pltpu.make_async_copy(back.at[stream, z], out_hbm.at[location_rows(z, stream)], own_sem.at[2 + stream])
        copy.start()
        own.append(copy)

    def out1_done(stream):
        own[2 + stream].wait()
        for step in range(1, NZ):
            source = lax.rem(z + step, NZ)
            arrived(out_hbm.at[location_rows(source, stream)], o1_recv.at[source, stream], at_z(source))

    text_products()
    pl.semaphore_wait(barrier, NZ - 1 + NQ - 1 + 1)
    text_send()
    in1_send(0)
    send(wp_hbm.at[half_rows], wp_far.at[half_rows], w_send.at[0], w_recv.at[0], pair)
    in1_send(1)
    send(wcp_hbm.at[quarter_rows], wcp_far.at[quarter_rows], w_send.at[2], w_recv.at[2], pair)
    text_core_sum()
    in1_done(0)
    in2_send(0)
    text_x_sum()
    in1_done(1)
    in2_send(1)
    text_z_sum()
    for n in (2, 3, 4):
        loads[n].wait()
    in2_done(0)
    temporal_norm(0)
    loads[5].wait()
    temporal(0)
    text_z_gather()
    arrived(wp_far.at[half_rows], w_recv.at[0], pair)
    send(wp_far.at[half_rows], wp_far.at[half_rows], w_send.at[1], w_recv.at[1], sibling)
    in2_done(1)
    temporal_norm(1)
    arrived(wcp_far.at[quarter_rows], w_recv.at[2], pair)
    send(wcp_far.at[quarter_rows], wcp_far.at[quarter_rows], w_send.at[4], w_recv.at[4], beside)
    send(wcp_far.at[quarter_rows], wcp_far.at[quarter_rows], w_send.at[3], w_recv.at[3], sibling)
    temporal(1)
    text_x_gather()
    loads[6].wait()
    loads[7].wait()
    arrived(wp_far.at[other_rows], w_recv.at[1], sibling)
    mix(0)
    loads[8].wait()
    text_core_gather()
    cross(0)
    arrived(wcp_far.at[beside_rows], w_recv.at[4], beside)
    send(wcp_far.at[beside_rows], wcp_far.at[beside_rows], w_send.at[5], w_recv.at[5], sibling)
    mix(1)
    for n in (3, 5):
        arrived(wcp_far.at[other_quarters[n // 4]], w_recv.at[n], sibling)
    out2_add(0)
    out2_send(0)
    cross(1)
    out2_add(1)
    out2_send(1)
    out2_done(0)
    out1_send(0)
    out2_done(1)
    out1_send(1)
    out1_done(0)
    out1_done(1)
    drain()


def mega(length, x, shift, scale, gate, wqkv, wp, wcq, wcp, ckv, te):
    bf16, f32 = jnp.bfloat16, jnp.float32
    dma, vmem = pltpu.SemaphoreType.DMA, pltpu.VMEM
    return pl.pallas_call(
        kernel,
        out_shape=jax.ShapeDtypeStruct((TOKENS, D), bf16),
        in_specs=[pl.BlockSpec(memory_space=pltpu.SMEM)] + [pl.BlockSpec(memory_space=pltpu.HBM)] * 10,
        out_specs=pl.BlockSpec(memory_space=pltpu.HBM),
        scratch_shapes=[
            vmem((D,), f32), vmem((D,), f32), vmem((D,), f32),
            vmem((2, 32, WIDTH), bf16), vmem((32, TEXT_LEN), bf16),
            vmem((3, WIDTH, D), bf16), vmem((WIDTH, D), bf16), vmem((WIDTH, D), bf16),
            vmem((WIDTH, D), bf16), vmem((WIDTH, D), bf16), vmem((WIDTH, D), bf16),
            vmem((NZ, 2, 16, D), bf16), vmem((128, 128), f32), vmem((128, 128), f32), vmem((256, 128), f32),
            vmem((2, NQ, 16, LOW), bf16), vmem((2, NQ, 16, LOW), bf16),
            vmem((FRAMES, D), bf16), vmem((3, WIDTH, FRAMES), f32), vmem((2, WIDTH, FRAMES), f32),
            vmem((2, 2, WIDTH, FRAMES), bf16), vmem((2, 2, WIDTH, FRAMES), bf16),
            vmem((2, FRAMES, D), f32), vmem((2, FRAMES, D), f32),
            vmem((2, NQ, 16, LOW), bf16), vmem((2, NQ, 16, LOW), bf16), vmem((2, NZ, 16, D), bf16),
            vmem((32, 384), bf16), vmem((192, 16, 128), bf16), vmem((96, 16, 128), bf16), vmem((96, 16, 128), bf16),
            vmem((8, 12, 16, 128), bf16), vmem((24, 8, 128), f32), vmem((8, 3, 8, 128), f32), vmem((24, 8, 128), f32),
            vmem((192, 16, 128), bf16),
            vmem((TEXT_ROWS, WIDTH), bf16), vmem((640, 384), f32),
            dma((9,)), dma((6,)), dma((6,)), dma((7, 2)), dma((8, 2)), dma((2, 16)), dma((2, 16)),
            dma((2, 2, 2)), dma((2, 2, 2)), dma((2, 16)), dma((2, 16)), dma((7, 2)), dma((8, 2)),
            dma((2,)), dma((2,)), dma((2, 8)), dma((2, 8)), dma((2, 8)), dma((2, 8)), dma((4,)),
        ],
        compiler_params=pltpu.CompilerParams(
            collective_id=0, has_side_effects=True, vmem_limit_bytes=60 * 1024 * 1024
        ),
        cost_estimate=pl.CostEstimate(flops=4_000_000_000, bytes_accessed=12_000_000, transcendentals=2_000_000),
        name="stdit",
    )(length, x, shift, scale, gate, wqkv, wp, wcq, wcp, ckv, te)


def body(
    video_latent, shift_temporal, scale_temporal, gate_temporal, temporal_qkv, temporal_proj,
    cross_query, cross_kv, cross_proj, text_embed, text_length,
):
    out = mega(
        text_length, video_latent.reshape(TOKENS, D),
        shift_temporal, scale_temporal, gate_temporal,
        jnp.transpose(temporal_qkv, (1, 2, 0)), temporal_proj, cross_query.T, cross_proj, cross_kv, text_embed.T,
    )
    return video_latent.astype(jnp.float32) + out.reshape(1, TOKENS, D).astype(jnp.float32)


def solution(mesh):
    return jax.shard_map(
        body,
        mesh=mesh,
        in_specs=(
            P("seq", None, None), P(), P(), P(), P(None, None, "tp"), P("tp", None), P(None, "tp"),
            P(None, "seq", "tp"), P("tp", None), P(None, "seq"), P(),
        ),
        out_specs=P("seq", None, None),
        check_vma=False,
    )
```

```python
import jax
import jax.numpy as jnp
from jax import lax
from jax.experimental import pallas as pl
from jax.experimental.pallas import tpu as pltpu
from jax.sharding import PartitionSpec as P

D = 1152
HD = 72
HEADS = 8
WIDTH = HEADS * HD
TOKENS = 256
FRAMES = 128
LOW, HIGH = 640, 512
NZ = 8
NQ = 16
TEXT_LEN = 300
TEXT_ROWS = 304
EXP_SCALE = HD ** (-0.5) * 1.4426950408889634
MESH = pl.DeviceIdType.MESH


def rows_of(index, size):
    return pl.ds(pl.multiple_of(index * size, size), size)


def dot(a, b, dims):
    return lax.dot_general(a, b, (dims, ((), ())), preferred_element_type=jnp.float32)


def attend(scores_of, value_of, visible, target, after):
    for group in range(0, HEADS, 4):
        scores = [scores_of(head) for head in range(group, group + 4)]
        weights, totals = [], []
        for score in scores:
            if visible is not None:
                score = jnp.where(visible, score, -1e30)
            top = jnp.max(score, axis=0, keepdims=True)
            weight = jnp.exp2((score - top) * EXP_SCALE)
            totals.append(1.0 / jnp.sum(weight, axis=0, keepdims=True))
            weights.append(weight.astype(jnp.bfloat16))
        mixed = [dot(value_of(group + n), weights[n], ((1,), (0,))) * totals[n] for n in range(4)]
        for n in (0, 2):
            target[(group + n) * HD : (group + n + 2) * HD] = jnp.concatenate(mixed[n : n + 2], axis=0).astype(jnp.bfloat16)
        after(group // 4)


def kernel(
    length_ref, x_hbm, shift_hbm, scale_hbm, gate_hbm, wqkv_hbm, wp_hbm, wcq_hbm, wcp_hbm, ckv_hbm, te_hbm,
    out_hbm,
    shift_ref, scale_ref, gate_ref, ckv_ref, te_ref, wqkv, wp, wp_far, wcq, wcp, wcp_far,
    s1, t32, u32, v32, msg, xin, normed, qkv, asked, att, att_far, branch, partial, om, o2, back,
    te_pad, part, core_in, part_x, x_in, part_z, z_in, z_full, full, tk, tv,
    load_sem, w_send, w_recv, s1_send, s1_recv, s2_send, s2_recv,
    a_send, a_recv, o2_send, o2_recv, o1_send, o1_recv,
    c_send, c_recv, x_send, x_recv, z_send, z_recv, own_sem,
):
    seq, hi = lax.axis_index("seq"), lax.axis_index("tp")
    z, q = seq // NQ, lax.rem(seq, NQ)
    core, spot = lax.rem(q, 2), q // 2

    def other_y(index):
        return index + 2 - 4 * lax.rem(index // 2, 2)

    def group_of(index):
        return index + hi * (other_y(index) - index)

    def place_of(index):
        group = group_of(index)
        return lax.rem(group, 2) * 8 + group // 2

    def at_z(index):
        return (index * NQ + q, hi)

    def at_q(index):
        return (z * NQ + index, hi)

    def at_spot(index):
        return at_q(2 * index + core)

    pair = (z * NQ + other_y(q), 1 - hi)
    sibling = at_q(q + 1 - 2 * core)

    barrier = pltpu.get_barrier_semaphore()
    for step in range(1, NZ):
        pl.semaphore_signal(barrier, inc=1, device_id=at_z(lax.rem(z + step, NZ)), device_id_type=MESH)
    for step in range(1, NQ):
        pl.semaphore_signal(barrier, inc=1, device_id=at_q(lax.rem(q + step, NQ)), device_id_type=MESH)
    pl.semaphore_signal(barrier, inc=1, device_id=pair, device_id_type=MESH)

    loads = [
        pltpu.make_async_copy(source, target, load_sem.at[n])
        for n, (source, target) in enumerate(
            (
                (te_hbm, te_ref), (ckv_hbm, ckv_ref), (shift_hbm, shift_ref), (scale_hbm, scale_ref),
                (gate_hbm, gate_ref), (wqkv_hbm, wqkv), (wp_hbm, wp), (wcq_hbm, wcq), (wcp_hbm, wcp),
            )
        )
    ]
    for load in loads:
        load.start()

    def remote(source, target, send, recv, device):
        return pltpu.make_async_remote_copy(
            src_ref=source, dst_ref=target, send_sem=send, recv_sem=recv, device_id=device, device_id_type=MESH
        )

    sent = []

    def send(source, target, send_sem, recv_sem, device, when=None):
        copy = remote(source, target, send_sem, recv_sem, device)
        if when is None:
            copy.start()
        else:
            pl.when(when)(copy.start)
        sent.append((copy, when))

    def arrived(target, recv_sem, device, when=None):
        copy = remote(target, target, c_send.at[0], recv_sem, device)
        if when is None:
            copy.wait_recv()
        else:
            pl.when(when)(copy.wait_recv)

    def drain():
        for copy, when in sent:
            if when is None:
                copy.wait_send()
            else:
                pl.when(when)(copy.wait_send)
        sent.clear()

    def text_products():
        loads[0].wait()
        loads[1].wait()
        te_pad[...] = jnp.zeros_like(te_pad)
        te_pad[:, :TEXT_LEN] = te_ref[...]
        part[190:] = jnp.zeros((2, 16, 128), jnp.bfloat16)
        for which in range(2):
            product = lax.dot_general(
                te_pad[:, :TEXT_ROWS], ckv_ref[which], (((0,), (0,)), ((), ())), preferred_element_type=jnp.float32
            ).astype(jnp.bfloat16)
            product = jnp.concatenate([product, jnp.zeros((TEXT_ROWS, 64), jnp.bfloat16)], axis=1)
            for r in range(TEXT_ROWS // 16):
                for tile in range(5):
                    part[r * 10 + which * 5 + tile] = product[r * 16 : r * 16 + 16, tile * 128 : tile * 128 + 128]

    def text_send():
        send(part.at[pl.ds(96 - 96 * core, 96)], core_in, c_send.at[0], c_recv.at[0], sibling)

    def text_core_sum():
        arrived(core_in, c_recv.at[0], sibling)
        part_x[...] = (part[pl.ds(96 * core, 96)].astype(jnp.float32) + core_in[...].astype(jnp.float32)).astype(jnp.bfloat16)
        for step in (4, 6, 2, 5, 3, 7, 1):
            target = lax.rem(spot + step, 8)
            send(part_x.at[pl.ds(12 * target, 12)], x_in.at[spot], x_send.at[0, step], x_recv.at[0, spot], at_spot(target))

    def text_x_sum():
        total = part_x[pl.ds(12 * spot, 12)].astype(jnp.float32)
        for step in range(1, 8):
            source = lax.rem(spot + step, 8)
            arrived(x_in.at[source], x_recv.at[0, source], at_spot(source))
            total += x_in[source].astype(jnp.float32)
        part_z[...] = total.reshape(24, 8, 128)
        for step in (4, 3, 5, 2, 6, 1, 7):
            target = lax.rem(z + step, NZ)
            send(part_z.at[pl.ds(3 * target, 3)], z_in.at[z], z_send.at[0, step], z_recv.at[0, z], at_z(target))

    def text_z_sum():
        total = part_z[pl.ds(3 * z, 3)]
        for step in range(1, NZ):
            source = lax.rem(z + step, NZ)
            arrived(z_in.at[source], z_recv.at[0, source], at_z(source))
            total += z_in[source]
        mine = z_full.at[pl.ds(3 * z, 3)]
        mine[...] = total
        for step in (4, 3, 5, 2, 6, 1, 7):
            send(mine, mine, z_send.at[1, step], z_recv.at[1, z], at_z(lax.rem(z + step, NZ)))

    def text_z_gather():
        for step in range(1, NZ):
            source = lax.rem(z + step, NZ)
            arrived(z_full.at[pl.ds(3 * source, 3)], z_recv.at[1, source], at_z(source))
        mine = full.at[pl.ds(96 * core + 12 * spot, 12)]
        mine[...] = z_full[...].reshape(12, 16, 128).astype(jnp.bfloat16)
        for step in (4, 6, 2, 5, 3, 7, 1):
            send(mine, mine, x_send.at[1, step], x_recv.at[1, spot], at_spot(lax.rem(spot + step, 8)))

    def text_x_gather():
        for step in range(1, 8):
            source = lax.rem(spot + step, 8)
            arrived(full.at[pl.ds(96 * core + 12 * source, 12)], x_recv.at[1, source], at_spot(source))
        mine = full.at[pl.ds(96 * core, 96)]
        send(mine, mine, c_send.at[1], c_recv.at[1], sibling)

    def text_core_gather():
        arrived(full.at[pl.ds(96 - 96 * core, 96)], c_recv.at[1], sibling)
        for tile in range(5):
            width = min(128, WIDTH - tile * 128)
            rows = []
            for r in range(TEXT_ROWS // 16):
                tk[r * 16 : r * 16 + 16, tile * 128 : tile * 128 + width] = full[r * 10 + tile][:, :width]
                rows.append(full[r * 10 + 5 + tile].astype(jnp.float32))
            rows.append(jnp.zeros((384 - TEXT_ROWS, 128), jnp.float32))
            tv[tile * 128 : (tile + 1) * 128] = jnp.concatenate(rows, axis=0).T

    half_rows = pl.ds(pl.multiple_of(core * 288, 288), 288)
    odd_x = lax.rem(q // 4, 2)
    beside = at_q(q + 4 - 8 * odd_x)
    quarter_rows = pl.ds(pl.multiple_of(core * 288 + odd_x * 144, 16), 144)
    beside_rows = pl.ds(pl.multiple_of(core * 288 + 144 - odd_x * 144, 16), 144)
    other_quarters = [
        pl.ds(pl.multiple_of(288 - core * 288 + start, 16), 144) for start in (odd_x * 144, 144 - odd_x * 144)
    ]
    other_rows = pl.ds(pl.multiple_of(288 - core * 288, 288), 288)
    own = []

    def location_rows(index, stream):
        return pl.ds(pl.multiple_of(index * 32 + stream * 16, 16), 16)

    def in1_send(stream):
        for n, step in enumerate((4, 3, 5, 2, 6, 1, 7)):
            target = lax.rem(z + step, NZ)
            send(
                x_hbm.at[location_rows(target, stream)],
                s1.at[z, stream], s1_send.at[n, stream], s1_recv.at[z, stream], at_z(target),
            )
        copy = pltpu.make_async_copy(x_hbm.at[location_rows(z, stream)], s1.at[z, stream], own_sem.at[stream])
        copy.start()
        own.append(copy)

    def in1_done(stream):
        own[stream].wait()
        for step in range(1, NZ):
            source = lax.rem(z + step, NZ)
            arrived(s1.at[source, stream], s1_recv.at[source, stream], at_z(source))

    def in2_send(stream):
        def spread_in(tile, carry):
            lanes = pl.ds(pl.multiple_of(tile * 128, 128), 128)
            upper = pl.ds(pl.multiple_of(lax.rem(tile + 5, 9) * 128, 128), 128)
            for n in range(NZ):
                t32[n * 16 : (n + 1) * 16] = s1[n, stream, :, lanes].astype(jnp.float32)
                u32[n * 16 : (n + 1) * 16] = s1[n, stream, :, upper].astype(jnp.float32)
            for n in range(NQ):
                both = jnp.concatenate([t32[pl.ds(n, 8, stride=16), :], u32[pl.ds(n, 8, stride=16), :]], axis=0)
                msg[stream, n, :, lanes] = both.astype(jnp.bfloat16)
            return carry

        lax.fori_loop(0, 5, spread_in, 0)
        for step in (8, 4, 12, 10, 6, 14, 2, 9, 5, 13, 11, 7, 15, 3, 1):
            dest = lax.rem(q + step, NQ)
            send(msg.at[stream, place_of(dest)], xin.at[stream, q], s2_send.at[stream, step], s2_recv.at[stream, q], at_q(dest))
        xin[stream, q] = msg[stream, place_of(q)]

    def in2_done(stream):
        for step in range(1, NQ):
            source = lax.rem(q + step, NQ)
            arrived(xin.at[stream, source], s2_recv.at[stream, source], at_q(source))

    def latent_rows(stream, n):
        first, second = xin[stream, 2 * n].astype(jnp.float32), xin[stream, 2 * n + 1].astype(jnp.float32)
        low = jnp.concatenate([first[:8], second[:8]], axis=0)
        high = jnp.concatenate([first[8:, :HIGH], second[8:, :HIGH]], axis=0)
        return jnp.concatenate([low, high], axis=1)

    def temporal_norm(stream):
        def norm_rows(n, carry):
            values = latent_rows(stream, n)
            center = jnp.mean(values, axis=-1, keepdims=True)
            values = values - center
            spread = jnp.mean(jnp.square(values), axis=-1, keepdims=True)
            values = values * lax.rsqrt(spread + 1e-06) * (1.0 + scale_ref[...].reshape(1, D)) + shift_ref[...].reshape(1, D)
            normed[rows_of(n, 16)] = values.astype(jnp.bfloat16)
            return carry

        lax.fori_loop(0, 8, norm_rows, 0, unroll=2)

    def head_rows(which, head):
        return qkv[which, head * HD : (head + 1) * HD].astype(jnp.bfloat16)

    def temporal(stream):
        def project(n, carry):
            qkv[n] = dot(wqkv[n], normed[...], ((1,), (1,)))
            return carry

        lax.fori_loop(0, 3, project, 0)
        attend(
            lambda head: dot(head_rows(1, head), head_rows(0, head), ((0,), (0,))),
            lambda head: head_rows(2, head), None, att.at[0, stream], lambda half: swap(0, stream, half),
        )

    def swap(kind, stream, half):
        rows = pl.ds(half * 288, 288)
        send(
            att.at[kind, stream, rows], att_far.at[kind, stream, rows],
            a_send.at[kind, stream, half], a_recv.at[kind, stream, half], pair,
        )

    def swapped(kind, stream):
        for half in range(2):
            arrived(att_far.at[kind, stream, pl.ds(half * 288, 288)], a_recv.at[kind, stream, half], pair)

    def mix(stream):
        branch[stream] = dot(att[0, stream], wp[...], ((0,), (0,)))
        swapped(0, stream)
        total = branch[stream] + dot(att_far[0, stream], wp_far[...], ((0,), (0,)))
        branch[stream] = total * gate_ref[...].reshape(1, D)

        def mix_rows(n, carry):
            rows = rows_of(n, 16)
            normed[rows] = (latent_rows(stream, n) + branch[stream, rows]).astype(jnp.bfloat16)
            return carry

        lax.fori_loop(0, 8, mix_rows, 0, unroll=2)
        asked[stream] = dot(wcq[...], normed[...], ((1,), (1,)))

    def cross(stream):
        row = lax.broadcasted_iota(jnp.int32, (TEXT_ROWS, FRAMES), 0)

        def scores_of(head):
            low, high = head * HD, (head + 1) * HD
            start, end = low // 128 * 128, min(-(-high // 128) * 128, WIDTH)
            place = lax.broadcasted_iota(jnp.int32, (end - start, FRAMES), 0) + start
            query = jnp.where((place >= low) & (place < high), asked[stream, start:end], 0.0).astype(jnp.bfloat16)
            return dot(tk[:, start:end], query, ((1,), (0,)))

        def value_of(head):
            return tv[head * HD : (head + 1) * HD, :TEXT_ROWS].astype(jnp.bfloat16)

        attend(scores_of, value_of, row < length_ref[0], att.at[1, stream], lambda half: swap(1, stream, half))
        partial[stream] = dot(att[1, stream], wcp[...], ((0,), (0,)))

    def fold(rows):
        high = jnp.concatenate([rows[:, LOW:], jnp.zeros((8, LOW - HIGH), jnp.float32)], axis=1)
        return jnp.concatenate([rows[:, :LOW], high], axis=0)

    def out2_add(stream):
        swapped(1, stream)
        partial[stream] += dot(att_far[1, stream], wcp_far[...], ((0,), (0,)))

        def add_rows(n, carry):
            om[stream, n] = fold(branch[stream, rows_of(n, 8)] + partial[stream, rows_of(n, 8)]).astype(jnp.bfloat16)
            return carry

        lax.fori_loop(0, NQ, add_rows, 0, unroll=2)

    def out2_send(stream):
        place = place_of(q)
        for first in range(2):
            for step in (4, 6, 2, 5, 3, 7, 1, 0):
                dest = 2 * lax.rem(spot + step, 8) + first
                when = None if step else core != first
                send(
                    om.at[stream, dest], o2.at[stream, place],
                    o2_send.at[stream, first * 8 + step], o2_recv.at[stream, place], at_q(dest), when,
                )
        o2[stream, place] = om[stream, q]

    def out2_done(stream):
        for step in range(1, NQ):
            source = lax.rem(q + step, NQ)
            arrived(o2.at[stream, place_of(source)], o2_recv.at[stream, place_of(source)], at_q(source))

    def out1_send(stream):
        def spread_out(tile, carry):
            lanes = pl.ds(pl.multiple_of(tile * 128, 128), 128)
            for n in range(NQ):
                v32[n * 16 : (n + 1) * 16] = o2[stream, n, :, lanes].astype(jnp.float32)
            for n in range(NZ):
                back[stream, n, :, lanes] = v32[pl.ds(n, 16, stride=16), :].astype(jnp.bfloat16)

            @pl.when(tile < 4)
            def _():
                upper = pl.ds(pl.multiple_of(tile * 128 + LOW, 128), 128)
                for n in range(NZ):
                    back[stream, n, :, upper] = v32[pl.ds(n + 8, 16, stride=16), :].astype(jnp.bfloat16)

            return carry

        lax.fori_loop(0, 5, spread_out, 0)
        for n, step in enumerate((4, 3, 5, 2, 6, 1, 7)):
            target = lax.rem(z + step, NZ)
            send(
                back.at[stream, target], out_hbm.at[location_rows(z, stream)],
                o1_send.at[n, stream], o1_recv.at[z, stream], at_z(target),
            )
        copy = pltpu.make_async_copy(back.at[stream, z], out_hbm.at[location_rows(z, stream)], own_sem.at[2 + stream])
        copy.start()
        own.append(copy)

    def out1_done(stream):
        own[2 + stream].wait()
        for step in range(1, NZ):
            source = lax.rem(z + step, NZ)
            arrived(out_hbm.at[location_rows(source, stream)], o1_recv.at[source, stream], at_z(source))

    text_products()
    pl.semaphore_wait(barrier, NZ - 1 + NQ - 1 + 1)
    text_send()
    in1_send(0)
    send(wp_hbm.at[half_rows], wp_far.at[half_rows], w_send.at[0], w_recv.at[0], pair)
    in1_send(1)
    send(wcp_hbm.at[quarter_rows], wcp_far.at[quarter_rows], w_send.at[2], w_recv.at[2], pair)
    text_core_sum()
    in1_done(0)
    in2_send(0)
    text_x_sum()
    in1_done(1)
    in2_send(1)
    text_z_sum()
    for n in (2, 3, 4):
        loads[n].wait()
    in2_done(0)
    temporal_norm(0)
    loads[5].wait()
    text_z_gather()
    temporal(0)
    arrived(wp_far.at[half_rows], w_recv.at[0], pair)
    send(wp_far.at[half_rows], wp_far.at[half_rows], w_send.at[1], w_recv.at[1], sibling)
    in2_done(1)
    temporal_norm(1)
    arrived(wcp_far.at[quarter_rows], w_recv.at[2], pair)
    send(wcp_far.at[quarter_rows], wcp_far.at[quarter_rows], w_send.at[4], w_recv.at[4], beside)
    send(wcp_far.at[quarter_rows], wcp_far.at[quarter_rows], w_send.at[3], w_recv.at[3], sibling)
    temporal(1)
    text_x_gather()
    loads[6].wait()
    loads[7].wait()
    arrived(wp_far.at[other_rows], w_recv.at[1], sibling)
    mix(0)
    loads[8].wait()
    text_core_gather()
    cross(0)
    arrived(wcp_far.at[beside_rows], w_recv.at[4], beside)
    send(wcp_far.at[beside_rows], wcp_far.at[beside_rows], w_send.at[5], w_recv.at[5], sibling)
    mix(1)
    for n in (3, 5):
        arrived(wcp_far.at[other_quarters[n // 4]], w_recv.at[n], sibling)
    out2_add(0)
    out2_send(0)
    cross(1)
    out2_add(1)
    out2_send(1)
    out2_done(0)
    out1_send(0)
    out2_done(1)
    out1_send(1)
    out1_done(0)
    out1_done(1)
    drain()


def mega(length, x, shift, scale, gate, wqkv, wp, wcq, wcp, ckv, te):
    bf16, f32 = jnp.bfloat16, jnp.float32
    dma, vmem = pltpu.SemaphoreType.DMA, pltpu.VMEM
    return pl.pallas_call(
        kernel,
        out_shape=jax.ShapeDtypeStruct((TOKENS, D), bf16),
        in_specs=[pl.BlockSpec(memory_space=pltpu.SMEM)] + [pl.BlockSpec(memory_space=pltpu.HBM)] * 10,
        out_specs=pl.BlockSpec(memory_space=pltpu.HBM),
        scratch_shapes=[
            vmem((D,), f32), vmem((D,), f32), vmem((D,), f32),
            vmem((2, 32, WIDTH), bf16), vmem((32, TEXT_LEN), bf16),
            vmem((3, WIDTH, D), bf16), vmem((WIDTH, D), bf16), vmem((WIDTH, D), bf16),
            vmem((WIDTH, D), bf16), vmem((WIDTH, D), bf16), vmem((WIDTH, D), bf16),
            vmem((NZ, 2, 16, D), bf16), vmem((128, 128), f32), vmem((128, 128), f32), vmem((256, 128), f32),
            vmem((2, NQ, 16, LOW), bf16), vmem((2, NQ, 16, LOW), bf16),
            vmem((FRAMES, D), bf16), vmem((3, WIDTH, FRAMES), f32), vmem((2, WIDTH, FRAMES), f32),
            vmem((2, 2, WIDTH, FRAMES), bf16), vmem((2, 2, WIDTH, FRAMES), bf16),
            vmem((2, FRAMES, D), f32), vmem((2, FRAMES, D), f32),
            vmem((2, NQ, 16, LOW), bf16), vmem((2, NQ, 16, LOW), bf16), vmem((2, NZ, 16, D), bf16),
            vmem((32, 384), bf16), vmem((192, 16, 128), bf16), vmem((96, 16, 128), bf16), vmem((96, 16, 128), bf16),
            vmem((8, 12, 16, 128), bf16), vmem((24, 8, 128), f32), vmem((8, 3, 8, 128), f32), vmem((24, 8, 128), f32),
            vmem((192, 16, 128), bf16),
            vmem((TEXT_ROWS, WIDTH), bf16), vmem((640, 384), f32),
            dma((9,)), dma((6,)), dma((6,)), dma((7, 2)), dma((8, 2)), dma((2, 16)), dma((2, 16)),
            dma((2, 2, 2)), dma((2, 2, 2)), dma((2, 16)), dma((2, 16)), dma((7, 2)), dma((8, 2)),
            dma((2,)), dma((2,)), dma((2, 8)), dma((2, 8)), dma((2, 8)), dma((2, 8)), dma((4,)),
        ],
        compiler_params=pltpu.CompilerParams(
            collective_id=0, has_side_effects=True, vmem_limit_bytes=60 * 1024 * 1024
        ),
        cost_estimate=pl.CostEstimate(flops=4_000_000_000, bytes_accessed=12_000_000, transcendentals=2_000_000),
        name="stdit",
    )(length, x, shift, scale, gate, wqkv, wp, wcq, wcp, ckv, te)


def body(
    video_latent, shift_temporal, scale_temporal, gate_temporal, temporal_qkv, temporal_proj,
    cross_query, cross_kv, cross_proj, text_embed, text_length,
):
    out = mega(
        text_length, video_latent.reshape(TOKENS, D),
        shift_temporal, scale_temporal, gate_temporal,
        jnp.transpose(temporal_qkv, (1, 2, 0)), temporal_proj, cross_query.T, cross_proj, cross_kv, text_embed.T,
    )
    return video_latent.astype(jnp.float32) + out.reshape(1, TOKENS, D).astype(jnp.float32)


def solution(mesh):
    return jax.shard_map(
        body,
        mesh=mesh,
        in_specs=(
            P("seq", None, None), P(), P(), P(), P(None, None, "tp"), P("tp", None), P(None, "tp"),
            P(None, "seq", "tp"), P("tp", None), P(None, "seq"), P(),
        ),
        out_specs=P("seq", None, None),
        check_vma=False,
    )
```
